32 devices in a mesh: rep: 4 (over z), fsdp: 8 (over y, x, core).
Axes of the slice: x: 2, y: 2, z: 4, core: 2. Of those that a mesh axis runs over, the one named last changes fastest.
Arguments:
- tokens: bfloat16 [40960, 1024], P(('rep', 'fsdp')), may hold values from -6 to 6
- item_lengths: int32 [32, 3], P(('rep', 'fsdp')), may hold values from 1 to 1024, 1280 in all within a row
- attn_gain: bfloat16 [1024], P('fsdp'), may hold values from 0.25 to 1.75
- attn_shift: bfloat16 [1024], P('fsdp'), may hold values from -4 to 4
- w_qkv: bfloat16 [1024, 3072], P('fsdp'), may hold values from -0.1875 to 0.1875
- rel_table: bfloat16 [32, 16], P('fsdp'), may hold values from -4 to 4
- w_out: bfloat16 [1024, 1024], P('fsdp'), may hold values from -0.5 to 0.5
- ffn_gain: bfloat16 [1024], P('fsdp'), may hold values from 0.25 to 1.75
- ffn_shift: bfloat16 [1024], P('fsdp'), may hold values from -4 to 4
- w_up: bfloat16 [1024, 4096], P('fsdp'), may hold values from -0.1875 to 0.1875
- up_bias: bfloat16 [4096], P('fsdp'), may hold values from -6 to 6
- w_down: bfloat16 [4096, 1024], P('fsdp'), may hold values from -0.09375 to 0.09375
- down_bias: bfloat16 [1024], P('fsdp'), may hold values from -6 to 6
- cotangent: bfloat16 [40960, 1024], P(('rep', 'fsdp')), may hold values from -6 to 6
Outputs:
- output: bfloat16 [40960, 1024], P(('rep', 'fsdp'))
- grad_tokens: bfloat16 [40960, 1024], P(('rep', 'fsdp'))
- grad_attn_gain: float32 [1024], P('fsdp')
- grad_attn_shift: float32 [1024], P('fsdp')
- grad_w_qkv: float32 [1024, 3072], P('fsdp')
- grad_rel_table: float32 [32, 16], P('fsdp')
- grad_w_out: float32 [1024, 1024], P('fsdp')
- grad_ffn_gain: float32 [1024], P('fsdp')
- grad_ffn_shift: float32 [1024], P('fsdp')
- grad_w_up: float32 [1024, 4096], P('fsdp')
- grad_up_bias: float32 [4096], P('fsdp')
- grad_w_down: float32 [4096, 1024], P('fsdp')
- grad_down_bias: float32 [1024], P('fsdp')
The draws below stay inside these ranges and needn't reach their ends.
Inputs may be any that keep to these rules, and one draw needn't show every extreme that they name: `item_lengths`: each device's row lists the lengths of its 3 items in order; they sum to 1280 and the longest is exactly 1024.
All inputs are finite; a program needn't handle non-finite values.
Results may differ from the reference program's by a relative error of at most 0.019.
Values may be sent and summed in bfloat16 or wider, within the bound.
No kernel may reach another device: no remote copies, remote signals or barrier semaphores. Data moves between devices by JAX's collectives and lax.ppermute only.
A program may use at most 320 MiB of HBM per device.

```python
import math
import jax
import jax.numpy as jnp
import numpy as np
from jax import lax

D = 1024
H = 16
HD = 64
FF = 4096
NBUCKET = 32
MAXDIST = 128
ITEMS = 3
TOK_DEV = 1280
LONGEST = 1024
TOKENS = 40960
DEVICES = 32


def levels(stream_key, extent, split, smallest, largest):
    def one(axis_at, shards_of):
        heights = jax.random.uniform(jax.random.fold_in(jax.random.fold_in(stream_key, 6), axis_at), (shards_of,), jnp.float32, smallest / len(split), largest / len(split))
        return jnp.repeat(jnp.exp(heights), extent[axis_at] // shards_of).reshape((-1,) + (1,) * (len(extent) - axis_at - 1))

    loudness = one(*split[0])
    for cut in split[1:]:
        loudness = loudness * one(*cut)
    return loudness


def profile(count, total, reach, slope):
    loads = [(1 << 20) // math.isqrt(standing ** slope) + 1 for standing in range(2, count + 1)]
    spare, holding = total - reach - (count - 1), [1] * (count - 1)
    while spare > 0:
        free = [i for i in range(count - 1) if holding[i] < reach]
        mass, budget = sum([loads[i] for i in free]), spare
        for i in free:
            extra = min(reach - holding[i], max(1, budget * loads[i] // mass), spare)
            holding[i] = holding[i] + extra
            spare = spare - extra
    return np.array([reach] + holding)


def uneven(key, count, total, most, lean):
    if count == 2:
        one = jax.random.randint(key, (), max(1, total - most), min(most, total - 1) + 1)
        return jnp.stack([one, total - one])
    lengths = jnp.asarray(profile(count, total, most, lean), jnp.int32)
    twos = (count - 1) // 2
    giver, sink = lengths[1:1 + 2 * twos:2], lengths[2:2 + 2 * twos:2]
    slack = jnp.minimum(giver - 1, most - sink)
    passed = jax.random.randint(jax.random.fold_in(key, 1), (twos,), 0, 1 << 20) % (slack + 1)
    lengths = lengths.at[1:1 + 2 * twos:2].set(giver - passed).at[2:2 + 2 * twos:2].set(sink + passed)
    return lengths[jax.random.permutation(jax.random.fold_in(key, 2), count)]


def scatter_about(key, extent, width, limit, cuts=(), kind=jnp.bfloat16):
    values = jax.random.normal(key, extent, jnp.float32) * width
    if len(cuts) > 0:
        values = levels(key, extent, cuts, -0.22, 0.18) * values
    return jnp.clip(values, min=-limit, max=limit).astype(kind)


def setup_inputs(seed: int = 0) -> dict:
    streams_of = jax.random.split(jax.random.key(seed), 15)
    return {
        "tokens": scatter_about(streams_of[0], (TOKENS, D), 1.0, 6.0, ((0, 32),)),
        "item_lengths": jax.vmap(lambda own: uneven(own, ITEMS, TOK_DEV, LONGEST, 2))(jax.random.split(streams_of[1], DEVICES)).reshape((DEVICES, ITEMS)).astype(jnp.int32),
        "attn_gain": jnp.clip(1.0 + 0.15 * jax.random.normal(streams_of[2], (D,), jnp.float32), 0.25, 1.75).astype(jnp.bfloat16),
        "attn_shift": scatter_about(streams_of[3], (D,), 0.3, 4.0, ((0, 8),)),
        "w_qkv": scatter_about(streams_of[4], (D, 3 * D), D ** -0.5, 0.1875, ((0, 8),)),
        "rel_table": scatter_about(streams_of[5], (NBUCKET, H), 1.0, 4.0, ((0, 8),)),
        "w_out": scatter_about(streams_of[6], (D, D), (D // 8) ** -0.5, 0.5, ((0, 8),)),
        "ffn_gain": jnp.clip(1.0 + 0.15 * jax.random.normal(streams_of[7], (D,), jnp.float32), 0.25, 1.75).astype(jnp.bfloat16),
        "ffn_shift": scatter_about(streams_of[8], (D,), 0.3, 4.0, ((0, 8),)),
        "w_up": scatter_about(streams_of[9], (D, FF), D ** -0.5, 0.1875, ((0, 8),)),
        "up_bias": scatter_about(streams_of[10], (FF,), 0.5, 6.0, ((0, 8),)),
        "w_down": scatter_about(streams_of[11], (FF, D), FF ** -0.5, 0.09375, ((0, 8),)),
        "down_bias": scatter_about(streams_of[12], (D,), 0.5, 6.0, ((0, 8),)),
        "cotangent": scatter_about(streams_of[13], (TOKENS, D), 1.0, 6.0, ((0, 32),)),
    }


@jax.custom_vjp
def low(v):
    return lax.optimization_barrier(v.astype(jnp.bfloat16)).astype(jnp.float32)

@jax.custom_vjp
def low_back(v):
    return v

def low_keep(v):
    return (low(v), None)

def low_pass(kept, grad):
    return (grad,)

def back_keep(v):
    return (v, None)

def back_low(kept, grad):
    return (low(grad),)
low.defvjp(low_keep, low_pass)
low_back.defvjp(back_keep, back_low)

def layer_norm(values, gain, shift):
    center = values - lax.optimization_barrier(jnp.mean(values, axis=-1, keepdims=True))
    spread = lax.optimization_barrier(jnp.mean(center * center, axis=-1, keepdims=True))
    return center * lax.rsqrt(spread + 1e-05) * gain + shift

def matmul(left, right):
    return jnp.dot(left, right, precision=lax.Precision.HIGHEST, preferred_element_type=jnp.float32)

def bucket_edges(bucket_count, reach_max):
    exact_count = bucket_count // 2
    edge_list = list(range(1, exact_count + 1))
    distance = np.arange(exact_count, 64 * reach_max)
    level_of = exact_count + np.floor(np.log(distance / exact_count) / np.log(reach_max / exact_count) * (bucket_count - exact_count)).astype(np.int64)
    for bucket_id in range(exact_count + 1, bucket_count):
        edge_list.append(int(distance[np.argmax(level_of >= bucket_id)]))
    return edge_list

def bucket_of(distance):
    bucket = jnp.zeros(distance.shape, jnp.int32)
    for edge_value in bucket_edges(NBUCKET, MAXDIST):
        bucket = bucket + (distance >= edge_value).astype(jnp.int32)
    return bucket

def forward(hidden_in, seg_ids, params):
    attn_gain, attn_shift, w_qkv, rel_table, w_out, ffn_gain, ffn_shift, w_up, up_bias, w_down, down_bias = params
    row_count = hidden_in.shape[0]
    normed = low(layer_norm(hidden_in, attn_gain, attn_shift))
    packed = low_back(low(matmul(normed, w_qkv)))
    queries = packed[:, :D].reshape(row_count, H, HD)
    keys_all = packed[:, D:2 * D].reshape(row_count, H, HD)
    values = packed[:, 2 * D:].reshape(row_count, H, HD)
    positions = jnp.arange(row_count, dtype=jnp.int32)
    distance = positions[:, None] - positions[None, :]
    allowed = (seg_ids[:, None] == seg_ids[None, :]) & (distance >= 0)
    rel_bias = jnp.transpose(rel_table[bucket_of(distance)], (2, 0, 1))
    scores = jnp.einsum('qhd,khd->hqk', queries, keys_all, precision=lax.Precision.HIGHEST) * 0.125 + rel_bias
    scores = jnp.where(allowed[None], low_back(scores), -1000000000.0)
    row_max = lax.optimization_barrier(jnp.max(scores, axis=-1, keepdims=True))
    exp_terms = jnp.where(allowed[None], jnp.exp(scores - row_max), 0.0)
    probs = low(exp_terms / lax.optimization_barrier(jnp.sum(exp_terms, axis=-1, keepdims=True)))
    mixed = jnp.einsum('hqk,khd->qhd', probs, values, precision=lax.Precision.HIGHEST).reshape(row_count, D)
    mixed = low_back(low(mixed))
    attended = low_back(matmul(mixed, w_out))
    middle = hidden_in + attended
    normed_two = low(layer_norm(middle, ffn_gain, ffn_shift))
    pre_act = low_back(matmul(normed_two, w_up) + up_bias)
    activ = low(jax.nn.gelu(pre_act, approximate=True))
    return middle + low_back(matmul(activ, w_down) + down_bias)

def reference(tokens, item_lengths, attn_gain, attn_shift, w_qkv, rel_table, w_out, ffn_gain, ffn_shift, w_up, up_bias, w_down, down_bias, cotangent):
    params = tuple((weight.astype(jnp.float32) for weight in (attn_gain, attn_shift, w_qkv, rel_table, w_out, ffn_gain, ffn_shift, w_up, up_bias, w_down, down_bias)))
    row_blocks = tokens.astype(jnp.float32).reshape(DEVICES, TOK_DEV, D)
    cot_blocks = cotangent.astype(jnp.float32).reshape(DEVICES, TOK_DEV, D)

    def accumulate(summed, inputs):
        block_rows, block_cot, lengths_row = inputs
        item_ends = jnp.cumsum(lengths_row).astype(jnp.int32)
        positions = jnp.arange(TOK_DEV, dtype=jnp.int32)
        seg_ids = lax.optimization_barrier(jnp.sum((positions[:, None] >= item_ends[None, :]).astype(jnp.int32), axis=1))
        result, pullback = jax.vjp(lambda rows_in, weights: forward(rows_in, seg_ids, weights), block_rows, params)
        grad_rows, grad_params = pullback(block_cot)
        summed = jax.tree.map(lambda left, right: left + right, summed, grad_params)
        return (summed, (result.astype(jnp.bfloat16), grad_rows.astype(jnp.bfloat16)))
    zero_init = jax.tree.map(jnp.zeros_like, params)
    summed, (outputs, grad_inputs) = lax.scan(accumulate, zero_init, (row_blocks, cot_blocks, item_lengths))
    grad_attn_gain, grad_attn_shift, grad_w_qkv, grad_rel_table, grad_w_out, grad_ffn_gain, grad_ffn_shift, grad_w_up, grad_up_bias, grad_w_down, grad_down_bias = summed
    return (outputs.reshape(TOKENS, D), grad_inputs.reshape(TOKENS, D), grad_attn_gain, grad_attn_shift, grad_w_qkv, grad_rel_table, grad_w_out, grad_ffn_gain, grad_ffn_shift, grad_w_up, grad_up_bias, grad_w_down, grad_down_bias)
```

```python
import jax
import jax.numpy as jnp
import numpy as np
from jax import lax
from jax.experimental import pallas as pl
from jax.experimental.pallas import tpu as pltpu
from jax.sharding import PartitionSpec as P

D = 1024
H = 16
HD = 64
NBUCKET = 32
MAXDIST = 128
bf16=jnp.bfloat16; f32=jnp.float32
NEG=-1e9
LONG=1024; SHORT=256; T=1280
NN=(((1,),(0,)),((),())); NT=(((1,),(1,)),((),())); TN=(((0,),(0,)),((),()))
def dot(a,b,dims): return lax.dot_general(a,b,dims,preferred_element_type=f32)
def split3(x):
    a=x.astype(bf16); r=x-a.astype(f32); b=r.astype(bf16); c=(r-b.astype(f32)).astype(bf16)
    return a,b,c

def fwd_body(bnd_ref,g_ref,q_ref,k_ref,v_ref,o_ref,qa_ref):
    lane=lax.broadcasted_iota(jnp.int32,(1,128),1)
    bnd=bnd_ref[0]
    r1=lax.broadcasted_iota(jnp.int32,(128,256),0); c1=lax.broadcasted_iota(jnp.int32,(128,256),1)
    outs=[]
    for h in range(2):
        mine=(lane<64) if h==0 else (lane>=64)
        base=64 if h==0 else 0
        g=g_ref[0,h:h+1,:]
        band=pltpu.roll(jnp.broadcast_to(g,(128,256)),0,1,stride=1,stride_axis=0)
        band=jnp.where(c1-128>r1,NEG,band)
        parts=[]; qas=[]
        for blk in range(5):
            R=256*blk
            lo=0 if blk<4 else 1024
            qrow=q_ref[R:R+256,:]*bf16(0.125)
            qm=jnp.where(mine,qrow,bf16(0))
            s=dot(qm,k_ref[lo:R+256,:],NT)
            nk=R+256-lo
            pieces=[]
            for sub in range(2):
                e=nk-256+128*(sub+1)
                rows=s[128*sub:128*sub+128]
                def mask(x,c0):
                    if blk<4: return x
                    rr=lax.broadcasted_iota(jnp.int32,x.shape,0)+128*sub
                    cc=lax.broadcasted_iota(jnp.int32,x.shape,1)+c0
                    return jnp.where((rr>=bnd)&(cc<bnd),NEG,x)
                segs=[]
                if e>=256:
                    if e>256: segs.append(rows[:,:e-256])
                    segs.append(mask(rows[:,e-256:e]+band,e-256))
                else:
                    segs.append(mask(rows[:,:128]+band[:,128:],0))
                m=None
                for sg in segs:
                    for c in range(0,sg.shape[1],128):
                        t=sg[:,c:c+128]
                        m=t if m is None else jnp.maximum(m,t)
                m=jnp.max(m,axis=1,keepdims=True)
                ps=[jnp.exp(sg-m).astype(bf16) for sg in segs]
                if e<nk: ps.append(jnp.zeros((128,nk-e),bf16))
                pieces.append((jnp.concatenate(ps,axis=1) if len(ps)>1 else ps[0],m))
            p=jnp.concatenate([pieces[0][0],pieces[1][0]],axis=0)
            m=jnp.concatenate([pieces[0][1],pieces[1][1]],axis=0)
            va=jnp.where(mine,v_ref[lo:R+256,:],jnp.where(lane==base,bf16(1),bf16(0)))
            o=dot(p,va,NN)
            l=o[:,base:base+1]
            parts.append(o*(1.0/l))
            a,b,c=split3(m+jnp.log(l))
            qas.append(jnp.where(mine,qrow,jnp.where(lane==base,a,jnp.where(lane==base+1,b,jnp.where(lane==base+2,c,bf16(0))))))
        for blk in range(5): qa_ref[256*blk:256*blk+256,128*h:128*h+128]=qas[blk]
        outs.append(parts)
    for blk in range(5):
        o_ref[256*blk:256*blk+256,:]=jnp.where(lane<64,outs[0][blk],outs[1][blk]).astype(bf16)

def attn_fwd(packed,g,bnd):
    return pl.pallas_call(fwd_body,
        grid=(8,),
        in_specs=[pl.BlockSpec(memory_space=pltpu.SMEM),
                  pl.BlockSpec((1,2,256),lambda i:(i,0,0)),
                  pl.BlockSpec((T,128),lambda i:(0,i)),
                  pl.BlockSpec((T,128),lambda i:(0,8+i)),
                  pl.BlockSpec((T,128),lambda i:(0,16+i))],
        out_specs=[pl.BlockSpec((T,128),lambda i:(0,i)),pl.BlockSpec((T,256),lambda i:(0,i))],
        out_shape=[jax.ShapeDtypeStruct((T,1024),bf16),jax.ShapeDtypeStruct((T,2048),bf16)],
        cost_estimate=pl.CostEstimate(flops=2*16*11*65536*128,bytes_accessed=16<<20,transcendentals=16*11*65536),
        compiler_params=pltpu.CompilerParams(vmem_limit_bytes=48<<20))(bnd,g,packed,packed,packed)

def bwd_body(bnd_ref,g_ref,qa_ref,k_ref,v_ref,o_ref,do_ref,gq_ref,gk_ref,gv_ref,gs_ref,dq_acc,band_acc):
    lane=lax.broadcasted_iota(jnp.int32,(1,128),1)
    bnd=bnd_ref[0]
    r1=lax.broadcasted_iota(jnp.int32,(128,256),0); c1=lax.broadcasted_iota(jnp.int32,(128,256),1)
    prod=do_ref[...].astype(f32)*o_ref[...].astype(f32)
    ph=prod.astype(bf16); plo=(prod-ph.astype(f32)).astype(bf16)
    i0=lax.broadcasted_iota(jnp.int32,(128,128),0); j0=lax.broadcasted_iota(jnp.int32,(128,128),1)
    sw=jnp.where((i0<64)!=(j0<64),bf16(1),bf16(0))
    delta=-(dot(ph,sw,NN)+dot(plo,sw,NN))
    dh,dl,_=split3(delta)
    gks=[];gvs=[]
    for h in range(2):
        mine=(lane<64) if h==0 else (lane>=64)
        base=64 if h==0 else 0
        g=g_ref[0,h:h+1,:]
        band=pltpu.roll(jnp.broadcast_to(g,(128,256)),0,1,stride=1,stride_axis=0)
        band=jnp.where(c1<r1,NEG,band)
        dob=do_ref[...]
        doa=jnp.where(mine,dob,jnp.where(lane==base,dh,jnp.where(lane==base+1,dl,bf16(0))))
        gk=[];gv=[]
        for blk in (3,2,1,0,4):
            R=256*blk
            hi=1024 if blk<4 else 1280
            nq=hi-R
            neg=jnp.where((lane>=base)&(lane<base+3),bf16(-1),bf16(0))
            one=jnp.where((lane>=base)&(lane<base+2),bf16(1),bf16(0))
            ka=jnp.where(mine,k_ref[R:R+256,:],neg)
            va=jnp.where(mine,v_ref[R:R+256,:],one)
            qa=qa_ref[R:hi,128*h:128*h+128]
            do=doa[R:hi]
            st=dot(ka,qa,NT)
            dpt=dot(va,do,NT)
            pr=[];dr=[]
            for sub in range(2):
                b0=128*sub
                w=min(256,nq-b0)
                sb=st[b0:b0+128,b0:b0+w]+band[:,:w]
                if blk==4:
                    rr=lax.broadcasted_iota(jnp.int32,sb.shape,0)+b0
                    cc=lax.broadcasted_iota(jnp.int32,sb.shape,1)+b0
                    sb=jnp.where((cc>=bnd)&(rr<bnd),NEG,sb)
                pb=jnp.exp(sb)
                db=pb*dpt[b0:b0+128,b0:b0+w]
                if h==0 or True:
                    if blk==3 and sub==0: band_acc[...]=db
                    elif w==256: band_acc[...]+=db
                    else: band_acc[:,:w]+=db
                ps=[pb.astype(bf16)]; ds=[db.astype(bf16)]
                if sub==1:
                    ps.insert(0,jnp.zeros((128,128),bf16)); ds.insert(0,jnp.zeros((128,128),bf16))
                if b0+w<nq:
                    pf=jnp.exp(st[b0:b0+128,b0+w:])
                    df=pf*dpt[b0:b0+128,b0+w:]
                    ps.append(pf.astype(bf16)); ds.append(df.astype(bf16))
                pr.append(jnp.concatenate(ps,axis=1) if len(ps)>1 else ps[0])
                dr.append(jnp.concatenate(ds,axis=1) if len(ds)>1 else ds[0])
            p=jnp.concatenate(pr,axis=0); ds=jnp.concatenate(dr,axis=0)
            gvb=dot(p,do,NN); gkb=dot(ds,qa,NN)
            dqb=dot(ds,ka,TN)
            if blk in (3,2,1,0):
                dq_acc[h,R:R+256,:]=dqb[:256]
                if nq>256: dq_acc[h,R+256:hi,:]+=dqb[256:]
            else:
                dq_acc[h,R:hi,:]=dqb
            gk.append((R,gkb)); gv.append((R,gvb))
        gks.append(gk);gvs.append(gv)
        Y=band_acc[...]
        n=64
        while n>=1:
            Y=Y[:n]+pltpu.roll(Y[n:2*n],256-n,1)
            n//=2
        gs_ref[0,h:h+1,:]=Y
    for (R,a),(_,b) in zip(*gks): gk_ref[R:R+256,:]=jnp.where(lane<64,a,b).astype(bf16)
    for (R,a),(_,b) in zip(*gvs): gv_ref[R:R+256,:]=jnp.where(lane<64,a,b).astype(bf16)
    gq_ref[...]=(jnp.where(lane<64,dq_acc[0],dq_acc[1])*0.125).astype(bf16)

def attn_bwd(packed,qa,o,do,g,bnd):
    sp=lambda off: pl.BlockSpec((T,128),lambda i:(0,off+i))
    sh=jax.ShapeDtypeStruct((T,1024),bf16)
    return pl.pallas_call(bwd_body,
        grid=(8,),
        in_specs=[pl.BlockSpec(memory_space=pltpu.SMEM),
                  pl.BlockSpec((1,2,256),lambda i:(i,0,0)),
                  pl.BlockSpec((T,256),lambda i:(0,i)),sp(8),sp(16),sp(0),sp(0)],
        out_specs=[sp(0),sp(0),sp(0),pl.BlockSpec((1,2,256),lambda i:(i,0,0))],
        out_shape=[sh,sh,sh,jax.ShapeDtypeStruct((8,2,256),f32)],
        scratch_shapes=[pltpu.VMEM((2,T,128),f32),pltpu.VMEM((128,256),f32)],
        cost_estimate=pl.CostEstimate(flops=5*16*11*65536*128,bytes_accessed=24<<20,transcendentals=16*11*65536),
        compiler_params=pltpu.CompilerParams(vmem_limit_bytes=56<<20))(bnd,g,qa,packed,packed,o,do)


def bucket_edges(bucket_count, reach_max):
    exact_count = bucket_count // 2
    edge_list = list(range(1, exact_count + 1))
    distance = np.arange(exact_count, 64 * reach_max)
    level_of = exact_count + np.floor(
        np.log(distance / exact_count)
        / np.log(reach_max / exact_count)
        * (bucket_count - exact_count)
    ).astype(np.int64)
    for bucket_id in range(exact_count + 1, bucket_count):
        edge_list.append(int(distance[np.argmax(level_of >= bucket_id)]))
    return edge_list


EDGES = np.array(bucket_edges(NBUCKET, MAXDIST))
BUCKET = np.array([int(np.sum(n >= EDGES)) for n in range(256)])


def onehot_bucket(distance, live):
    hot = (np.arange(NBUCKET)[:, None] == BUCKET[distance][None, :]) & live[None, :]
    return hot.astype(np.float32)


def gelu_tanh(values):
    return jax.nn.gelu(values, approximate=True)


def norm_stats(values):
    mean = jnp.mean(values, axis=-1, keepdims=True)
    center = values - mean
    spread = jnp.mean(center * center, axis=-1, keepdims=True)
    return center * lax.rsqrt(spread + 1e-05), lax.rsqrt(spread + 1e-05)


def norm_back(xhat, rstd, scaled):
    return rstd * (
        scaled
        - jnp.mean(scaled, axis=-1, keepdims=True)
        - xhat * jnp.mean(scaled * xhat, axis=-1, keepdims=True)
    )


def local(
    tokens, item_lengths, attn_gain, attn_shift, w_qkv, rel_table, w_out,
    ffn_gain, ffn_shift, w_up, up_bias, w_down, down_bias, cotangent,
):
    gather = lambda a: lax.all_gather(a, "fsdp", axis=0, tiled=True)
    pieces = (attn_gain, attn_shift, ffn_gain, ffn_shift, down_bias, up_bias, rel_table.reshape(-1))
    small = jnp.concatenate(pieces).reshape(1, -1)
    small_full = gather(small)
    qkv_full = gather(w_qkv)
    out_full = gather(w_out)
    up_full = gather(w_up)
    down_full = gather(w_down)
    cuts = np.cumsum([0] + [piece.size for piece in pieces])
    ways = small_full.shape[0]
    part = lambda i: small_full[:, cuts[i] : cuts[i + 1]].reshape(-1).astype(jnp.float32)
    gain_one, shift_one, gain_two, shift_two, down_bias_full, up_bias_full = (
        part(i) for i in range(6)
    )
    table = part(6).reshape(NBUCKET, H)
    lens = item_lengths[0]
    first, second = lens[0], lens[1]
    long_first = first == LONG
    long_mid = second == LONG
    start = jnp.where(long_first, 0, jnp.where(long_mid, first, first + second))
    bound = jnp.where(long_first, second, jnp.where(long_mid, lens[2], first)).reshape(1)
    rotate = lambda a, by: jnp.roll(a, by, axis=0)
    tok = rotate(tokens, -start)
    cot = rotate(cotangent, -start)
    relative = table - table[NBUCKET - 1 :]
    reach = np.arange(256)
    fwd_hot = onehot_bucket(np.maximum(128 - reach, 0), reach <= 128)
    bwd_hot = onehot_bucket(reach, reach < 129)
    spread_of = lambda hot: jnp.dot(
        relative.T, hot, precision=lax.Precision.HIGHEST, preferred_element_type=jnp.float32
    ).reshape(8, 2, 256)
    bias_fwd, bias_bwd = spread_of(fwd_hot), spread_of(bwd_hot)

    hidden = tok.astype(jnp.float32)
    xhat_one, rstd_one = norm_stats(hidden)
    normed = (xhat_one * gain_one + shift_one).astype(jnp.bfloat16)
    packed = jnp.dot(normed, qkv_full, preferred_element_type=jnp.float32).astype(jnp.bfloat16)
    mixed, query_aug = attn_fwd(packed, bias_fwd, bound)
    middle = hidden + jnp.dot(mixed, out_full, preferred_element_type=jnp.float32)
    xhat_two, rstd_two = norm_stats(middle)
    normed_two = (xhat_two * gain_two + shift_two).astype(jnp.bfloat16)
    pre_act = (
        jnp.dot(normed_two, up_full, preferred_element_type=jnp.float32) + up_bias_full
    )
    activ = gelu_tanh(pre_act).astype(jnp.bfloat16)
    cot_float = cot.astype(jnp.float32)
    grad_w_down = jnp.einsum("tf,td->fd", activ, cot, preferred_element_type=jnp.float32)
    grad_down_bias = jnp.sum(cot_float, axis=0)
    scatter = lambda a: lax.psum_scatter(
        a.astype(jnp.bfloat16), "fsdp", scatter_dimension=0, tiled=True
    )
    share_down = scatter(grad_w_down)
    grad_activ = jnp.einsum("td,fd->tf", cot, down_full, preferred_element_type=jnp.float32)
    grad_pre = jax.vjp(gelu_tanh, pre_act)[1](grad_activ)[0].astype(jnp.bfloat16)
    grad_w_up = jnp.einsum("td,tf->df", normed_two, grad_pre, preferred_element_type=jnp.float32)
    share_up = scatter(grad_w_up)
    grad_up_bias = jnp.sum(grad_pre.astype(jnp.float32), axis=0)
    grad_normed_two = jnp.einsum("tf,df->td", grad_pre, up_full, preferred_element_type=jnp.float32)
    grad_ffn_gain = jnp.sum(grad_normed_two * xhat_two, axis=0)
    grad_ffn_shift = jnp.sum(grad_normed_two, axis=0)
    grad_middle = cot_float + norm_back(xhat_two, rstd_two, grad_normed_two * gain_two)
    grad_attended = grad_middle.astype(jnp.bfloat16)
    grad_w_out = jnp.einsum("td,te->de", mixed, grad_attended, preferred_element_type=jnp.float32)
    share_out = scatter(grad_w_out)
    grad_mixed = jnp.einsum(
        "te,de->td", grad_attended, out_full, preferred_element_type=jnp.float32
    ).astype(jnp.bfloat16)
    gq, gk, gv, grad_reach = attn_bwd(packed, query_aug, mixed, grad_mixed, bias_bwd, bound)
    grad_packed = jnp.concatenate([gq, gk, gv], axis=1)
    near_hot = onehot_bucket(reach, reach < EDGES[-1])
    grad_near = jnp.dot(
        near_hot, grad_reach.reshape(H, 256).T,
        precision=lax.Precision.HIGHEST, preferred_element_type=jnp.float32,
    )
    far = (np.arange(NBUCKET) == NBUCKET - 1).astype(np.float32)[:, None]
    grad_rel_table = grad_near - far * jnp.sum(grad_near, axis=0, keepdims=True)
    grad_w_qkv = jnp.einsum("td,te->de", normed, grad_packed, preferred_element_type=jnp.float32)
    share_qkv = scatter(grad_w_qkv)
    grad_normed = jnp.einsum("te,de->td", grad_packed, qkv_full, preferred_element_type=jnp.float32)
    grad_attn_gain = jnp.sum(grad_normed * xhat_one, axis=0)
    grad_attn_shift = jnp.sum(grad_normed, axis=0)
    grad_tokens = (
        grad_middle + norm_back(xhat_one, rstd_one, grad_normed * gain_one)
    ).astype(jnp.bfloat16)
    grad_tokens = rotate(grad_tokens, start)
    ffn_out = jnp.dot(activ, down_full, preferred_element_type=jnp.float32) + down_bias_full
    output = rotate((middle + ffn_out).astype(jnp.bfloat16), start)

    flat = lambda a: a.reshape(ways, -1)
    vectors = jnp.concatenate(
        [
            flat(grad_attn_gain), flat(grad_attn_shift), flat(grad_ffn_gain),
            flat(grad_ffn_shift), flat(grad_down_bias), flat(grad_up_bias), flat(grad_rel_table),
        ],
        axis=1,
    )
    share_small = lax.psum_scatter(
        vectors.astype(jnp.bfloat16), "fsdp", scatter_dimension=0, tiled=True
    )
    total = lambda a: lax.psum(a, "rep").astype(jnp.float32)
    sum_small = total(share_small)
    cut = lambda i: sum_small[0, cuts[i] : cuts[i + 1]]
    return (
        output, grad_tokens, cut(0), cut(1), total(share_qkv), cut(6).reshape(-1, H),
        total(share_out), cut(2), cut(3), total(share_up), cut(5), total(share_down), cut(4),
    )


def solution(mesh):
    rows, vec, mat = P(("rep", "fsdp"), None), P("fsdp"), P("fsdp", None)
    in_specs = (rows, rows, vec, vec, mat, mat, mat, vec, vec, mat, vec, mat, vec, rows)
    out_specs = (rows, rows, vec, vec, mat, mat, mat, vec, vec, mat, vec, mat, vec)
    return jax.shard_map(local, mesh=mesh, in_specs=in_specs, out_specs=out_specs, check_vma=False)
```

```python
import functools

import jax
import jax.numpy as jnp
import numpy as np
from jax import lax
from jax.experimental import pallas as pl
from jax.experimental.pallas import tpu as pltpu
from jax.sharding import PartitionSpec as P

D = 1024
H = 16
HD = 64
FF = 4096
NBUCKET = 32
MAXDIST = 128
bf16 = jnp.bfloat16
f32 = jnp.float32
NEG = -1e9
LONG = 1024
SHORT = 256
T = 1280
NN = (((1,), (0,)), ((), ()))
NT = (((1,), (1,)), ((), ()))
TN = (((0,), (0,)), ((), ()))


def dot(a, b, dims):
    return lax.dot_general(a, b, dims, preferred_element_type=f32)


def split3(x):
    a = x.astype(bf16)
    r = x - a.astype(f32)
    b = r.astype(bf16)
    return a, b, (r - b.astype(f32)).astype(bf16)


def fwd_body(bnd_ref,g_ref,q_ref,k_ref,v_ref,o_ref,qa_ref):
    lane=lax.broadcasted_iota(jnp.int32,(1,128),1)
    bnd=bnd_ref[0]
    r1=lax.broadcasted_iota(jnp.int32,(128,256),0); c1=lax.broadcasted_iota(jnp.int32,(128,256),1)
    outs=[]
    for h in range(2):
        mine=(lane<64) if h==0 else (lane>=64)
        base=64 if h==0 else 0
        g=g_ref[0,h:h+1,:]
        band=pltpu.roll(jnp.broadcast_to(g,(128,256)),0,1,stride=1,stride_axis=0)
        band=jnp.where(c1-128>r1,NEG,band)
        parts=[]; qas=[]
        for blk in range(5):
            R=256*blk
            lo=0 if blk<4 else 1024
            qrow=q_ref[R:R+256,:]*bf16(0.125)
            qm=jnp.where(mine,qrow,bf16(0))
            s=dot(qm,k_ref[lo:R+256,:],NT)
            nk=R+256-lo
            pieces=[]
            for sub in range(2):
                e=nk-256+128*(sub+1)
                rows=s[128*sub:128*sub+128]
                def mask(x,c0):
                    if blk<4: return x
                    rr=lax.broadcasted_iota(jnp.int32,x.shape,0)+128*sub
                    cc=lax.broadcasted_iota(jnp.int32,x.shape,1)+c0
                    return jnp.where((rr>=bnd)&(cc<bnd),NEG,x)
                segs=[]
                if e>=256:
                    if e>256: segs.append(rows[:,:e-256])
                    segs.append(mask(rows[:,e-256:e]+band,e-256))
                else:
                    segs.append(mask(rows[:,:128]+band[:,128:],0))
                m=None
                for sg in segs:
                    for c in range(0,sg.shape[1],128):
                        t=sg[:,c:c+128]
                        m=t if m is None else jnp.maximum(m,t)
                m=jnp.max(m,axis=1,keepdims=True)
                ps=[jnp.exp(sg-m).astype(bf16) for sg in segs]
                if e<nk: ps.append(jnp.zeros((128,nk-e),bf16))
                pieces.append((jnp.concatenate(ps,axis=1) if len(ps)>1 else ps[0],m))
            p=jnp.concatenate([pieces[0][0],pieces[1][0]],axis=0)
            m=jnp.concatenate([pieces[0][1],pieces[1][1]],axis=0)
            va=jnp.where(mine,v_ref[lo:R+256,:],jnp.where(lane==base,bf16(1),bf16(0)))
            o=dot(p,va,NN)
            l=o[:,base:base+1]
            parts.append(o*(1.0/l))
            a,b,c=split3(m+jnp.log(l))
            qas.append(jnp.where(mine,qrow,jnp.where(lane==base,a,jnp.where(lane==base+1,b,jnp.where(lane==base+2,c,bf16(0))))))
        for blk in range(5): qa_ref[256*blk:256*blk+256,128*h:128*h+128]=qas[blk]
        outs.append(parts)
    for blk in range(5):
        o_ref[256*blk:256*blk+256,:]=jnp.where(lane<64,outs[0][blk],outs[1][blk]).astype(bf16)

def attn_fwd(packed,g,bnd):
    return pl.pallas_call(fwd_body,
        grid=(8,),
        in_specs=[pl.BlockSpec(memory_space=pltpu.SMEM),
                  pl.BlockSpec((1,2,256),lambda i:(i,0,0)),
                  pl.BlockSpec((T,128),lambda i:(0,i)),
                  pl.BlockSpec((T,128),lambda i:(0,8+i)),
                  pl.BlockSpec((T,128),lambda i:(0,16+i))],
        out_specs=[pl.BlockSpec((T,128),lambda i:(0,i)),pl.BlockSpec((T,256),lambda i:(0,i))],
        out_shape=[jax.ShapeDtypeStruct((T,1024),bf16),jax.ShapeDtypeStruct((T,2048),bf16)],
        cost_estimate=pl.CostEstimate(flops=2*16*11*65536*128,bytes_accessed=16<<20,transcendentals=16*11*65536),
        compiler_params=pltpu.CompilerParams(vmem_limit_bytes=48<<20))(bnd,g,packed,packed,packed)

def bwd_body(bnd_ref,g_ref,qa_ref,k_ref,v_ref,o_ref,do_ref,grad_ref,gs_ref,dq_acc,band_acc):
    lane=lax.broadcasted_iota(jnp.int32,(1,128),1)
    bnd=bnd_ref[0]
    r1=lax.broadcasted_iota(jnp.int32,(128,256),0); c1=lax.broadcasted_iota(jnp.int32,(128,256),1)
    prod=do_ref[...].astype(f32)*o_ref[...].astype(f32)
    ph=prod.astype(bf16); plo=(prod-ph.astype(f32)).astype(bf16)
    i0=lax.broadcasted_iota(jnp.int32,(128,128),0); j0=lax.broadcasted_iota(jnp.int32,(128,128),1)
    sw=jnp.where((i0<64)!=(j0<64),bf16(1),bf16(0))
    delta=-(dot(ph,sw,NN)+dot(plo,sw,NN))
    dh,dl,_=split3(delta)
    gks=[];gvs=[]
    for h in range(2):
        mine=(lane<64) if h==0 else (lane>=64)
        base=64 if h==0 else 0
        g=g_ref[0,h:h+1,:]
        band=pltpu.roll(jnp.broadcast_to(g,(128,256)),0,1,stride=1,stride_axis=0)
        band=jnp.where(c1<r1,NEG,band)
        dob=do_ref[...]
        doa=jnp.where(mine,dob,jnp.where(lane==base,dh,jnp.where(lane==base+1,dl,bf16(0))))
        gk=[];gv=[]
        for blk in (3,2,1,0,4):
            R=256*blk
            hi=1024 if blk<4 else 1280
            nq=hi-R
            neg=jnp.where((lane>=base)&(lane<base+3),bf16(-1),bf16(0))
            one=jnp.where((lane>=base)&(lane<base+2),bf16(1),bf16(0))
            ka=jnp.where(mine,k_ref[R:R+256,:],neg)
            va=jnp.where(mine,v_ref[R:R+256,:],one)
            qa=qa_ref[R:hi,128*h:128*h+128]
            do=doa[R:hi]
            st=dot(ka,qa,NT)
            dpt=dot(va,do,NT)
            pr=[];dr=[]
            for sub in range(2):
                b0=128*sub
                w=min(256,nq-b0)
                sb=st[b0:b0+128,b0:b0+w]+band[:,:w]
                if blk==4:
                    rr=lax.broadcasted_iota(jnp.int32,sb.shape,0)+b0
                    cc=lax.broadcasted_iota(jnp.int32,sb.shape,1)+b0
                    sb=jnp.where((cc>=bnd)&(rr<bnd),NEG,sb)
                pb=jnp.exp(sb)
                db=pb*dpt[b0:b0+128,b0:b0+w]
                if h==0 or True:
                    if blk==3 and sub==0: band_acc[...]=db
                    elif w==256: band_acc[...]+=db
                    else: band_acc[:,:w]+=db
                ps=[pb.astype(bf16)]; ds=[db.astype(bf16)]
                if sub==1:
                    ps.insert(0,jnp.zeros((128,128),bf16)); ds.insert(0,jnp.zeros((128,128),bf16))
                if b0+w<nq:
                    pf=jnp.exp(st[b0:b0+128,b0+w:])
                    df=pf*dpt[b0:b0+128,b0+w:]
                    ps.append(pf.astype(bf16)); ds.append(df.astype(bf16))
                pr.append(jnp.concatenate(ps,axis=1) if len(ps)>1 else ps[0])
                dr.append(jnp.concatenate(ds,axis=1) if len(ds)>1 else ds[0])
            p=jnp.concatenate(pr,axis=0); ds=jnp.concatenate(dr,axis=0)
            gvb=dot(p,do,NN); gkb=dot(ds,qa,NN)
            dqb=dot(ds,ka,TN)
            if blk in (3,2,1,0):
                dq_acc[h,R:R+256,:]=dqb[:256]
                if nq>256: dq_acc[h,R+256:hi,:]+=dqb[256:]
            else:
                dq_acc[h,R:hi,:]=dqb
            gk.append((R,gkb)); gv.append((R,gvb))
        gks.append(gk);gvs.append(gv)
        Y=band_acc[...]
        n=64
        while n>=1:
            Y=Y[:n]+pltpu.roll(Y[n:2*n],256-n,1)
            n//=2
        gs_ref[0,h:h+1,:]=Y
    for (R,a),(_,b) in zip(*gks): grad_ref[1,R:R+256,:]=jnp.where(lane<64,a,b).astype(bf16)
    for (R,a),(_,b) in zip(*gvs): grad_ref[2,R:R+256,:]=jnp.where(lane<64,a,b).astype(bf16)
    grad_ref[0]=(jnp.where(lane<64,dq_acc[0],dq_acc[1])*0.125).astype(bf16)

def attn_bwd(packed,qa,o,do,g,bnd,half):
    sp=lambda off: pl.BlockSpec((T,128),lambda i:(0,off+4*half+i))
    return pl.pallas_call(bwd_body,
        grid=(4,),
        in_specs=[pl.BlockSpec(memory_space=pltpu.SMEM),
                  pl.BlockSpec((1,2,256),lambda i:(4*half+i,0,0)),
                  pl.BlockSpec((T,256),lambda i:(0,4*half+i)),sp(8),sp(16),sp(0),sp(0)],
        out_specs=[pl.BlockSpec((3,T,128),lambda i:(0,0,i)),pl.BlockSpec((1,2,256),lambda i:(i,0,0))],
        out_shape=[jax.ShapeDtypeStruct((3,T,512),bf16),jax.ShapeDtypeStruct((4,2,256),f32)],
        scratch_shapes=[pltpu.VMEM((2,T,128),f32),pltpu.VMEM((128,256),f32)],
        cost_estimate=pl.CostEstimate(flops=5*8*11*65536*128,bytes_accessed=12<<20,transcendentals=8*11*65536),
        compiler_params=pltpu.CompilerParams(vmem_limit_bytes=56<<20))(bnd,g,qa,packed,packed,o,do)


def shape(*dims, dtype=bf16):
    return jax.ShapeDtypeStruct(dims, dtype)


def whole(*dims):
    return pl.BlockSpec(dims, lambda i: (0,) * len(dims))


def columns(rows, width, first=0):
    return pl.BlockSpec((rows, width), lambda i: (0, first + i))


SCALAR = pl.BlockSpec(memory_space=pltpu.SMEM)


def call(body, grid, in_specs, out_specs, out_shape, scratch=(), flops=0, moved=0, aliases={}):
    if not flops:
        moved = 0
    return pl.pallas_call(
        body,
        grid=(grid,),
        in_specs=in_specs,
        out_specs=out_specs,
        out_shape=out_shape,
        scratch_shapes=list(scratch),
        input_output_aliases=aliases,
        cost_estimate=pl.CostEstimate(flops=flops, bytes_accessed=moved, transcendentals=0),
        compiler_params=pltpu.CompilerParams(vmem_limit_bytes=58 << 20),
    )


def row_stats(x):
    mean = jnp.mean(x, axis=-1, keepdims=True)
    center = x - mean
    rstd = lax.rsqrt(jnp.mean(center * center, axis=-1, keepdims=True) + 1e-05)
    return center * rstd, rstd


def back_through_norm(xhat, rstd, scaled):
    return rstd * (
        scaled
        - jnp.mean(scaled, axis=-1, keepdims=True)
        - xhat * jnp.mean(scaled * xhat, axis=-1, keepdims=True)
    )


def shifted_rows(ext, offset, r):
    fine = lax.rem(offset, 8)
    rows = ext[pl.ds(pl.multiple_of(offset - fine + r, 8), 136), :]
    return pltpu.roll(rows, lax.rem(136 - fine, 136), 0)[:128]


def prep_body(start_ref, tok_ref, cot_ref, tok_out, cot_out, bias_out, ext):
    start = start_ref[0]
    for source, target in ((tok_ref, tok_out), (cot_ref, cot_out)):
        for r in range(0, T, 256):
            ext[r : r + 256, :] = source[r : r + 256, :].astype(f32)
        ext[T : T + SHORT, :] = source[0:SHORT, :].astype(f32)
        total = None
        for r in range(0, T, 128):
            rows = shifted_rows(ext, start, r)
            target[r : r + 128, :] = rows.astype(bf16)
            if target is cot_out:
                part = jnp.sum(rows, axis=0, keepdims=True)
                total = part if total is None else total + part
    bias_out[...] = total


def prep(start, tokens, cotangent):
    return call(
        prep_body, 1,
        [SCALAR, whole(T, D), whole(T, D)],
        [whole(T, D), whole(T, D), whole(1, D)],
        [shape(T, D), shape(T, D), shape(1, D, dtype=f32)],
        [pltpu.VMEM((T + SHORT + 8, D), f32)],
        moved=11 << 20,
    )(start, tokens, cotangent)


def qkv_body(tok_ref, gain_ref, shift_ref, w_ref, packed_ref, normed_ref):
    @pl.when(pl.program_id(0) == 0)
    def _():
        for r in range(0, T, 256):
            xhat, _ = row_stats(tok_ref[r : r + 256, :].astype(f32))
            normed_ref[r : r + 256, :] = (xhat * gain_ref[...] + shift_ref[...]).astype(bf16)

    packed_ref[...] = dot(normed_ref[...], w_ref[...], NN).astype(bf16)


def qkv_forward(tok, gain, shift, w_qkv):
    return call(
        qkv_body, 6,
        [whole(T, D), whole(1, D), whole(1, D), columns(D, 512)],
        [columns(T, 512), whole(T, D)],
        [shape(T, 3 * D), shape(T, D)],
        flops=6 * T * D * D, moved=20 << 20,
    )(tok, gain, shift, w_qkv)


PIECES = (
    (0, 0, 128), (1, 0, 128), (2, 0, 128), (4, 0, 128), (6, 0, 64), (6, 64, 64),
    (3, 0, 128), (5, 0, 128), (7, 0, 64), (7, 64, 64),
)


def qkv_pieces_body(me_ref, tok_ref, gain_ref, shift_ref, *refs):
    pieces = refs[: len(PIECES)]
    packed_ref, normed_ref, w_out, w_all, arrived, left = refs[len(PIECES) :]
    step = pl.program_id(0)
    save = pltpu.make_async_copy(w_all, w_out, left)

    @pl.when(step == 0)
    def _():
        copies = []
        for n, (other, first, rows) in enumerate(PIECES):
            at = pl.multiple_of((me_ref[0] ^ other) * 128 + first, 64)
            copy = pltpu.make_async_copy(pieces[n], w_all.at[pl.ds(at, rows), :], arrived.at[n])
            copy.start()
            copies.append(copy)
        for r in range(0, T, 256):
            xhat, _ = row_stats(tok_ref[r : r + 256, :].astype(f32))
            normed_ref[r : r + 256, :] = (xhat * gain_ref[...] + shift_ref[...]).astype(bf16)
        for copy in copies:
            copy.wait()
        save.start()

    at = pl.multiple_of(step * 512, 512)
    packed_ref[...] = dot(normed_ref[...], w_all[:, pl.ds(at, 512)], NN).astype(bf16)

    @pl.when(step == pl.num_programs(0) - 1)
    def _():
        save.wait()


def qkv_forward_pieces(me, tok, gain, shift, pieces):
    anywhere = pl.BlockSpec(memory_space=pl.ANY)
    return call(
        qkv_pieces_body, 6,
        [SCALAR, whole(T, D), whole(1, D), whole(1, D)] + [anywhere] * len(PIECES),
        [columns(T, 512), whole(T, D), anywhere],
        [shape(T, 3 * D), shape(T, D), shape(D, 3 * D)],
        [
            pltpu.VMEM((D, 3 * D), bf16),
            pltpu.SemaphoreType.DMA((len(PIECES),)),
            pltpu.SemaphoreType.DMA,
        ],
        flops=6 * T * D * D, moved=26 << 20,
    )(me, tok, gain, shift, *pieces)


def out_body(mixed_ref, w_ref, tok_ref, gain_ref, shift_ref, middle_ref, normed_ref):
    middle = tok_ref[...].astype(f32) + dot(mixed_ref[...], w_ref[...], NN)
    middle_ref[...] = middle
    xhat, _ = row_stats(middle)
    normed_ref[...] = (xhat * gain_ref[...] + shift_ref[...]).astype(bf16)


def out_forward(mixed, w_out_up, tok, gain, shift):
    rows = pl.BlockSpec((256, D), lambda i: (i, 0))
    return call(
        out_body, T // 256,
        [rows, whole(D, D), rows, whole(1, D), whole(1, D)],
        [rows, rows],
        [shape(T, D, dtype=f32), shape(T, D)],
        flops=2 * T * D * D, moved=16 << 20,
    )(mixed, w_out_up, tok, gain, shift)


C0 = float(np.sqrt(2.0 / np.pi))
C1 = 0.044715 * C0


def up_body(normed_ref, w_ref, bias_ref, activ_ref, slope_ref):
    bias = bias_ref[...]
    for r in range(0, T, 256):
        u = dot(normed_ref[r : r + 256, :], w_ref[...], NN) + bias
        square = u * u
        half = 0.5 * jnp.tanh(u * (C0 + C1 * square)) + 0.5
        activ = u * half
        activ_ref[r : r + 256, :] = activ.astype(bf16)
        slope = half + activ * (1.0 - half) * (2.0 * C0 + 6.0 * C1 * square)
        slope_ref[r : r + 256, :] = slope.astype(bf16)


def up_forward(normed_two, w_out_up, up_bias):
    return call(
        up_body, 8,
        [whole(T, D), columns(D, 512, 2), columns(1, 512)],
        [columns(T, 512), columns(T, 512)],
        [shape(T, FF), shape(T, FF)],
        flops=2 * T * D * FF, moved=32 << 20,
    )(normed_two, w_out_up, up_bias)


def grad_down_body(activ_ref, cot_ref, out_ref):
    out_ref[0, 0] = dot(activ_ref[...], cot_ref[...], TN).astype(bf16).reshape(out_ref.shape[2:])


def ffn_shape(ways):
    return shape(ways, 2, 4, D // ways, D)


def grad_down(activ, cot, ways):
    rows = FF // ways
    return call(
        grad_down_body, ways,
        [columns(T, rows), whole(T, D)],
        pl.BlockSpec((1, 1, 4, D // ways, D), lambda i: (i, 0, 0, 0, 0)),
        ffn_shape(ways),
        flops=2 * T * D * FF, moved=21 << 20,
    )(activ, cot)


def grad_up_body(left_ref, right_ref, held_ref, out_ref):
    value = dot(left_ref[...], right_ref[...], TN).astype(bf16)
    out_ref[...] = value.reshape(out_ref.shape)


def grad_up(left, right, held, ways):
    return call(
        grad_up_body, 8,
        [whole(T, D), columns(T, 512), pl.BlockSpec(memory_space=pl.ANY)],
        pl.BlockSpec((ways, 1, 1, D // ways, 512), lambda i: (0, 1, i // 2, 0, i % 2)),
        ffn_shape(ways),
        flops=2 * T * D * FF, moved=21 << 20, aliases={2: 0},
    )(left, right, held)


def grad_pre_body(cot_ref, w_ref, slope_ref, pre_ref, bias_ref):
    total = None
    for r in range(0, T, 256):
        pre = (
            dot(cot_ref[r : r + 256, :], w_ref[...], NT) * slope_ref[r : r + 256, :].astype(f32)
        ).astype(bf16)
        pre_ref[r : r + 256, :] = pre
        part = jnp.sum(pre.astype(f32), axis=0, keepdims=True)
        total = part if total is None else total + part
    bias_ref[...] = total


def grad_pre_of(cot, w_down, slope):
    return call(
        grad_pre_body, 8,
        [whole(T, D), pl.BlockSpec((512, D), lambda i: (i, 0)), columns(T, 512)],
        [columns(T, 512), columns(1, 512)],
        [shape(T, FF), shape(1, FF, dtype=f32)],
        flops=2 * T * D * FF, moved=32 << 20,
    )(cot, w_down, slope)


def grad_tile_body(left_ref, right_ref, out_ref):
    right = right_ref[...]
    right = right.reshape(right.shape[-2:])
    out_ref[...] = dot(left_ref[...], right, TN).astype(bf16)


def right_tiles(right):
    if right.ndim == 3:
        return right.shape[0], pl.BlockSpec((1, T, 512), lambda i: (i, 0, 0))
    return right.shape[1] // 512, columns(T, 512)


def grad_columns(left, right):
    tiles, spec = right_tiles(right)
    return call(
        grad_tile_body, tiles,
        [whole(T, D), spec],
        columns(D, 512),
        shape(D, tiles * 512),
        flops=2 * T * D * tiles * 512, moved=T * (D + tiles * 512) * 2,
    )(left, right)


def take_blocks(me, left_ref, held, core):
    for rel in range(4):
        at = pl.multiple_of((((me >> 1) ^ rel) * 2 + core) * 128, 128)
        held[:, 128 * rel : 128 * rel + 128] = left_ref[:, pl.ds(at, 128)]


def tile_specs(lefts, rights):
    specs, begins, first = [SCALAR], [], 0
    for right in rights:
        if right.ndim == 3:
            count = right.shape[0]
            spec = pl.BlockSpec(
                (1, T, 512), lambda i, a=first, n=count: (jnp.clip(i - a, 0, n - 1), 0, 0)
            )
        else:
            count = right.shape[1] // 512
            spec = pl.BlockSpec(
                (T, 512), lambda i, a=first, n=count: (0, jnp.clip(i - a, 0, n - 1))
            )
        specs.append(spec)
        begins.append(first)
        first += count
    return specs + [whole(T, D)] * len(lefts), begins, first


def block_products(me, core, begins, total, lefts, rights, held, emit):
    step = pl.program_id(0)
    for begin, end, left_ref, right_ref in zip(begins, begins[1:] + [total], lefts, rights):

        @pl.when(step == begin)
        def _():
            take_blocks(me, left_ref, held, core)

        @pl.when((step >= begin) & (step < end))
        def _():
            right = right_ref[...]
            emit(dot(held[...], right.reshape(right.shape[-2:]), TN))


def grad_theirs(me, lefts, rights):
    specs, begins, tiles = tile_specs(lefts, rights)
    n = len(lefts)

    def body(me_ref, *refs):
        out_ref, held = refs[2 * n :]

        def emit(value):
            out_ref[...] = value.astype(bf16)

        me = me_ref[0]
        block_products(me, 1 - (me & 1), begins, tiles, refs[n : 2 * n], refs[:n], held, emit)

    return call(
        body, tiles, specs, columns(512, 512), shape(512, tiles * 512),
        [pltpu.VMEM((T, 512), bf16)],
        flops=T * D * tiles * 512, moved=T * (D + tiles * 512) * 2,
    )(me, *rights, *lefts)


def grad_mine(me, lefts, rights, other):
    specs, begins, tiles = tile_specs(lefts, rights)
    n = len(lefts)

    def body(me_ref, *refs):
        other_ref, a_send, a_keep, b_send, b_keep, held = refs[2 * n :]

        def emit(value):
            total = (value + other_ref[...].astype(f32)).astype(bf16)
            for rel, target, place in ((0, a_keep, 0), (1, a_send, 0), (2, a_keep, 1), (3, a_send, 1)):
                target[place] = total[128 * rel : 128 * rel + 128, :256]
            for rel, target, place in ((0, b_keep, 0), (1, b_keep, 1), (2, b_send, 0), (3, b_send, 1)):
                target[place] = total[128 * rel : 128 * rel + 128, 256:]

        me = me_ref[0]
        block_products(me, me & 1, begins, tiles, refs[n : 2 * n], refs[:n], held, emit)

    part = pl.BlockSpec((2, 128, 256), lambda i: (0, 0, i))
    return call(
        body, tiles, specs + [columns(512, 512)], [part] * 4, [shape(2, 128, tiles * 256)] * 4,
        [pltpu.VMEM((T, 512), bf16)],
        flops=T * D * tiles * 512, moved=T * (D + tiles * 512) * 2,
    )(me, *rights, *lefts, other)


def pair_sum_body(a_keep, a_got, b_keep, b_got, a_send, a_rest, b_send, b_rest):
    for keep, got, send, rest in ((a_keep, a_got, a_send, a_rest), (b_keep, b_got, b_send, b_rest)):
        for place, target in ((1, send), (0, rest)):
            target[...] = (keep[place].astype(f32) + got[place].astype(f32)).astype(bf16)


def pair_sum(*parts):
    width = parts[0].shape[2]
    return call(
        pair_sum_body, 1,
        [whole(2, 128, width)] * 4,
        [whole(128, width)] * 4,
        [shape(128, width)] * 4,
        moved=128 * width * 24,
    )(*parts)


def add(a_ref, b_ref):
    return a_ref[...].astype(f32) + b_ref[...].astype(f32)


def last_sum_body(place_ref, a_keep, a_got, b_keep, b_got, send, keep):
    bit = place_ref[0] & 1
    for n, (one, two) in enumerate(((a_keep, a_got), (b_keep, b_got))):
        for target, mine in ((keep, bit), (send, 1 - bit)):
            at = pl.ds(pl.multiple_of(mine * 64, 64), 64)
            total = (one[at, :].astype(f32) + two[at, :].astype(f32)).astype(bf16)
            for tile in range(total.shape[1] // 256):
                target[:, 512 * tile + 256 * n : 512 * tile + 256 * n + 256] = total[
                    :, 256 * tile : 256 * tile + 256
                ]


def last_sum(place, *parts):
    width = 2 * parts[0].shape[1]
    return call(
        last_sum_body, 1,
        [SCALAR] + [whole(128, width // 2)] * 4,
        [whole(64, width)] * 2,
        [shape(64, width)] * 2,
        moved=128 * width * 6,
    )(place, *parts)


def half_sum_body(place_ref, keep, got, send, rest):
    bit = place_ref[0] >> 1
    for target, mine in ((rest, bit), (send, 1 - bit)):
        at = pl.ds(pl.multiple_of(mine * 32, 32), 32)
        target[...] = (keep[at, :].astype(f32) + got[at, :].astype(f32)).astype(bf16)


def half_sum(place, keep, got):
    width = keep.shape[1]
    return call(
        half_sum_body, 1,
        [SCALAR] + [whole(64, width)] * 2,
        [whole(32, width)] * 2,
        [shape(32, width)] * 2,
        moved=64 * width * 6,
    )(place, keep, got)


def quarter_sum_body(keep, got, out):
    out[...] = add(keep, got).astype(bf16)


def quarter_sum(keep, got):
    width = keep.shape[1]
    return call(
        quarter_sum_body, 1, [whole(32, width)] * 2, whole(32, width), shape(32, width),
        moved=32 * width * 6,
    )(keep, got)


def widen_body(sum_ref, down_ref, up_ref):
    rows = sum_ref.shape[3]
    for k in range(4):
        down_ref[rows * k : rows * k + rows, :] = sum_ref[0, 0, k].astype(f32)
        up_ref[:, D * k : D * k + D] = sum_ref[0, 1, k].astype(f32)


def widen(total):
    rows = total.shape[3]
    return call(
        widen_body, 1,
        [whole(*total.shape)],
        [whole(4 * rows, D), whole(rows, FF)],
        [shape(4 * rows, D, dtype=f32), shape(rows, FF, dtype=f32)],
    )(total)


def spread_body(place_ref, low_own, low_next, low_far, high_own, high_next, high_far, qkv_out, out_out):
    one, two = place_ref[0] & 1, place_ref[0] >> 1
    for own, near, far, half in ((low_own, low_next, low_far, 0), (high_own, high_next, high_far, 1)):
        for ref, rows, bit_one, bit_two in (
            (own, slice(0, 32), one, two),
            (near, slice(0, 32), one, 1 - two),
            (far, slice(0, 32), 1 - one, two),
            (far, slice(32, 64), 1 - one, 1 - two),
        ):
            at = pl.ds(pl.multiple_of(bit_one * 64 + bit_two * 32, 32), 32)
            for n in range(3):
                first = 1024 * n + 512 * half
                qkv_out[at, first : first + 512] = ref[rows, 512 * n : 512 * n + 512].astype(f32)
            if half == 0:
                out_out[at, :] = ref[rows, 1536:].astype(f32)


def spread(place, *parts):
    return call(
        spread_body, 1,
        [SCALAR] + [whole(*part.shape) for part in parts],
        [whole(128, 3 * D), whole(128, D)],
        [shape(128, 3 * D, dtype=f32), shape(128, D, dtype=f32)],
        moved=128 * 4 * D * 6,
    )(place, *parts)


def mid_body(
    pre_ref, up_ref, middle_ref, cot_ref, gain_ref, w_out_ref,
    mid_ref, att_ref, mixed_ref, gain_out, shift_out, acc,
):
    step = pl.program_id(0)

    @pl.when(step == 0)
    def _():
        acc[...] = dot(pre_ref[...], up_ref[...], NT)

    @pl.when(step > 0)
    def _():
        acc[...] += dot(pre_ref[...], up_ref[...], NT)

    @pl.when(step == pl.num_programs(0) - 1)
    def _():
        gains = shifts = None
        for r in range(0, T, 256):
            g = acc[r : r + 256, :]
            xhat, rstd = row_stats(middle_ref[r : r + 256, :])
            a = jnp.sum(g * xhat, axis=0, keepdims=True)
            b = jnp.sum(g, axis=0, keepdims=True)
            gains = a if gains is None else gains + a
            shifts = b if shifts is None else shifts + b
            mid = cot_ref[r : r + 256, :].astype(f32) + back_through_norm(
                xhat, rstd, g * gain_ref[...]
            )
            mid_ref[r : r + 256, :] = mid
            att = mid.astype(bf16)
            att_ref[r : r + 256, :] = att
            mixed_ref[r : r + 256, :] = dot(att, w_out_ref[...], NT).astype(bf16)
        gain_out[...] = gains
        shift_out[...] = shifts


def grad_middle_of(grad_pre, w_out_up, middle, cot, gain):
    return call(
        mid_body, 8,
        [
            columns(T, 512), columns(D, 512, 2), whole(T, D), whole(T, D), whole(1, D),
            whole(D, D),
        ],
        [whole(T, D), whole(T, D), whole(T, D), whole(1, D), whole(1, D)],
        [
            shape(T, D, dtype=f32), shape(T, D), shape(T, D),
            shape(1, D, dtype=f32), shape(1, D, dtype=f32),
        ],
        [pltpu.VMEM((T, D), f32)],
        flops=2 * T * D * FF + 2 * T * D * D, moved=42 << 20,
    )(grad_pre, w_out_up, middle, cot, gain, w_out_up)


def unrotate(ext, start, out_ref):
    ext[0:SHORT, :] = ext[T : T + SHORT, :]
    for r in range(0, T, 128):
        out_ref[r : r + 128, :] = shifted_rows(ext, SHORT - start, r).astype(bf16)


def tok_body(
    start_ref, low_ref, high_ref, w_ref, tok_ref, mid_ref, gain_ref, grad_ref, gain_out, shift_out, ext
):
    step = pl.program_id(0)

    @pl.when(step == 0)
    def _():
        ext[SHORT : SHORT + T, :] = dot(low_ref[0], w_ref[...], NT)

    @pl.when((step > 0) & (lax.rem(step, 2) == 0))
    def _():
        ext[SHORT : SHORT + T, :] += dot(low_ref[0], w_ref[...], NT)

    @pl.when(lax.rem(step, 2) == 1)
    def _():
        ext[SHORT : SHORT + T, :] += dot(high_ref[0], w_ref[...], NT)

    @pl.when(step == pl.num_programs(0) - 1)
    def _():
        gains = shifts = None
        for r in range(0, T, 256):
            g = ext[SHORT + r : SHORT + r + 256, :]
            xhat, rstd = row_stats(tok_ref[r : r + 256, :].astype(f32))
            a = jnp.sum(g * xhat, axis=0, keepdims=True)
            b = jnp.sum(g, axis=0, keepdims=True)
            gains = a if gains is None else gains + a
            shifts = b if shifts is None else shifts + b
            ext[SHORT + r : SHORT + r + 256, :] = mid_ref[r : r + 256, :] + back_through_norm(
                xhat, rstd, g * gain_ref[...]
            )
        unrotate(ext, start_ref[0], grad_ref)
        gain_out[...] = gains
        shift_out[...] = shifts


def grad_tokens_of(start, low, high, w_qkv, tok, mid, gain):
    half = pl.BlockSpec((1, T, 512), lambda i: (i // 2, 0, 0))
    return call(
        tok_body, 6,
        [
            SCALAR, half, half, columns(D, 512), whole(T, D), whole(T, D), whole(1, D),
        ],
        [whole(T, D), whole(1, D), whole(1, D)],
        [shape(T, D), shape(1, D, dtype=f32), shape(1, D, dtype=f32)],
        [pltpu.VMEM((T + SHORT + 8, D), f32)],
    )(start, low, high, w_qkv, tok, mid, gain)


def output_body(start_ref, activ_ref, w_ref, middle_ref, bias_ref, out_ref, ext):
    step = pl.program_id(0)

    @pl.when(step == 0)
    def _():
        ext[SHORT : SHORT + T, :] = middle_ref[...] + bias_ref[...]

    ext[SHORT : SHORT + T, :] += dot(activ_ref[...], w_ref[...], NN)

    @pl.when(step == pl.num_programs(0) - 1)
    def _():
        unrotate(ext, start_ref[0], out_ref)


def output_of(start, activ, w_down, middle, bias):
    return call(
        output_body, 4,
        [
            SCALAR, columns(T, 1024), pl.BlockSpec((1024, D), lambda i: (i, 0)), whole(T, D),
            whole(1, D),
        ],
        whole(T, D),
        shape(T, D),
        [pltpu.VMEM((T + SHORT + 8, D), f32)],
    )(start, activ, w_down, middle, bias)


def bucket_edges(bucket_count, reach_max):
    exact_count = bucket_count // 2
    edge_list = list(range(1, exact_count + 1))
    distance = np.arange(exact_count, 64 * reach_max)
    level_of = exact_count + np.floor(
        np.log(distance / exact_count)
        / np.log(reach_max / exact_count)
        * (bucket_count - exact_count)
    ).astype(np.int64)
    for bucket_id in range(exact_count + 1, bucket_count):
        edge_list.append(int(distance[np.argmax(level_of >= bucket_id)]))
    return edge_list


EDGES = np.array(bucket_edges(NBUCKET, MAXDIST))
BUCKET = np.array([int(np.sum(n >= EDGES)) for n in range(256)])


def onehot_bucket(distance, live):
    hot = (np.arange(NBUCKET)[:, None] == BUCKET[distance][None, :]) & live[None, :]
    return hot.astype(np.float32)


def swap(a, bit):
    return lax.ppermute(a, "fsdp", [(i, i ^ bit) for i in range(8)])


def swap_rep(a, bit):
    return lax.ppermute(a, "rep", [(i, i ^ bit) for i in range(4)])


def gather_small(small):
    n = lax.axis_size("fsdp")
    if n != 8:
        return lax.all_gather(small, "fsdp", axis=0)
    me = lax.axis_index("fsdp")
    held = small[None]
    for bit in (1, 2, 4):
        other = swap(held, bit)
        upper = (me & bit) != 0
        held = jnp.concatenate(
            [jnp.where(upper, other, held), jnp.where(upper, held, other)], axis=0
        )
    return held


def after(value, *others):
    return lax.optimization_barrier((value,) + others)[0]


def after_all(values, *others):
    return lax.optimization_barrier(tuple(values) + others)[: len(values)]


def local(
    tokens, item_lengths, attn_gain, attn_shift, w_qkv, rel_table, w_out,
    ffn_gain, ffn_shift, w_up, up_bias, w_down, down_bias, cotangent,
):
    gather = lambda a: lax.all_gather(a, "fsdp", axis=0, tiled=True)
    pieces = (attn_gain, attn_shift, ffn_gain, ffn_shift, down_bias, up_bias, rel_table.reshape(-1))
    cuts = np.cumsum([0] + [piece.size for piece in pieces])
    rows = -(-int(cuts[-1]) // 2048) * 16
    small = jnp.concatenate(pieces + (jnp.zeros((rows * 128 - int(cuts[-1]),), bf16),))
    small_full = gather_small(small.reshape(rows, 128))
    ways = small_full.shape[0]
    small_full = small_full.reshape(ways, rows * 128)
    me = lax.axis_index("fsdp").astype(jnp.int32).reshape(1)
    by_pieces = ways == 8 and lax.axis_size("rep") == 4
    lens = item_lengths[0]
    first, second = lens[0], lens[1]
    long_first = first == LONG
    long_mid = second == LONG
    start = jnp.where(long_first, 0, jnp.where(long_mid, first, first + second)).reshape(1)
    bound = jnp.where(long_first, second, jnp.where(long_mid, lens[2], first)).reshape(1)
    tok, cot, grad_down_bias = prep(start, tokens, cotangent)
    out_up_own = jnp.concatenate([w_out, w_up], axis=1)
    if by_pieces:
        from_core, from_x, from_y = swap(w_qkv, 1), swap(w_qkv, 2), swap(w_qkv, 4)
        from_x, from_y = after_all((from_x, from_y), tok, out_up_own)
        top, bottom = swap(from_x[:64], 4), swap(from_y[64:], 2)
        out_up_own = after(out_up_own, top, bottom)
        qkv_pieces = (
            w_qkv, from_core, from_x, from_y, top, bottom,
            swap(from_x, 1), swap(from_y, 1), swap(top, 1), swap(bottom, 1),
        )
    out_up = gather(out_up_own)
    part = lambda i: small_full[:, cuts[i] : cuts[i + 1]].reshape(1, -1).astype(f32)
    gain_one, shift_one, gain_two, shift_two, down_bias_full, up_bias_full = (
        part(i) for i in range(6)
    )
    table = part(6).reshape(NBUCKET, H)
    relative = table - table[NBUCKET - 1 :]
    reach = np.arange(256)
    fwd_hot = onehot_bucket(np.maximum(128 - reach, 0), reach <= 128)
    bwd_hot = onehot_bucket(reach, reach < 129)
    spread_of = lambda hot: jnp.dot(
        relative.T, hot, precision=lax.Precision.HIGHEST, preferred_element_type=f32
    ).reshape(8, 2, 256)
    bias_fwd, bias_bwd = spread_of(fwd_hot), spread_of(bwd_hot)

    scatter = lambda a: lax.psum_scatter(a, "fsdp", scatter_dimension=0, tiled=True)
    total = lambda a: lax.psum(a, "rep")

    if by_pieces:
        qkv_pieces = after_all(qkv_pieces, bias_fwd, gain_two)
        packed, normed, qkv_full = qkv_forward_pieces(me, tok, gain_one, shift_one, qkv_pieces)
    else:
        qkv_full = gather(w_qkv)
        packed, normed = qkv_forward(tok, gain_one, shift_one, qkv_full)

    def begin(lefts, rights):
        return swap(grad_theirs(me, lefts, rights), 1)

    def second(lefts, rights, other):
        a_send, a_keep, b_send, b_keep = grad_mine(me, lefts, rights, other)
        return a_keep, swap(a_send, 2), b_keep, swap(b_send, 4)

    def third(parts):
        a_send, a_keep, b_send, b_keep = pair_sum(*parts)
        return a_keep, swap(a_send, 4), b_keep, swap(b_send, 2)

    place = lax.axis_index("rep").astype(jnp.int32).reshape(1)

    def along_one(parts):
        send, keep = last_sum(place, *parts)
        return keep, swap_rep(send, 1)

    def along_two(parts):
        send, keep = half_sum(place, *parts)
        return keep, swap_rep(send, 2)

    mixed, query_aug = attn_fwd(packed, bias_fwd, bound)
    down_full = gather(after(w_down, mixed, out_up))
    middle, normed_two = out_forward(mixed, out_up, tok, gain_two, shift_two)
    activ, slope = up_forward(normed_two, out_up, up_bias_full)
    grad_w_ffn = grad_down(activ, cot, ways)
    grad_pre, grad_up_bias = grad_pre_of(after(cot, grad_w_ffn), down_full, slope)
    grad_w_ffn = grad_up(normed_two, grad_pre, grad_w_ffn, ways)
    share_ffn = scatter(grad_w_ffn)
    grad_middle, grad_att, grad_mixed, grad_ffn_gain, grad_ffn_shift = grad_middle_of(
        after(grad_pre, grad_w_ffn), out_up, middle, cot, gain_two
    )
    low, reach_low = attn_bwd(packed, query_aug, mixed, grad_mixed, bias_bwd, bound, 0)
    if by_pieces:
        pair = (normed, mixed), (low, grad_att)
        low_other = begin(*pair)
        packed_next = after(packed, low_other)
    else:
        packed_next = after(packed, low)
    high, reach_high = attn_bwd(
        packed_next, query_aug, mixed, grad_mixed, bias_bwd, bound, 1
    )
    grad_reach = jnp.concatenate([reach_low, reach_high], axis=0)
    near_hot = onehot_bucket(reach, reach < EDGES[-1])
    grad_near = jnp.dot(
        near_hot, grad_reach.reshape(H, 256).T,
        precision=lax.Precision.HIGHEST, preferred_element_type=f32,
    )
    far = (np.arange(NBUCKET) == NBUCKET - 1).astype(np.float32)[:, None]
    grad_rel_table = grad_near - far * jnp.sum(grad_near, axis=0, keepdims=True)
    if by_pieces:
        high_other = begin((normed,), (high,))
        low_parts = second(pair[0], (low, after(grad_att, high_other)), low_other)
        high_parts = second((normed,), (after(high, low_parts[0]),), high_other)
        low_sent = low_parts[0]
        low_parts = third(low_parts)
        high_next = after(high, high_parts[0], low_parts[0])
    else:
        share_low = scatter(grad_columns(normed, low))
        share_high = scatter(grad_columns(normed, high))
        share_out = scatter(grad_columns(mixed, grad_att))
        low_sent = high_next = high
    grad_tokens, grad_attn_gain, grad_attn_shift = grad_tokens_of(
        start, low, high_next, qkv_full, tok, grad_middle, gain_one
    )
    flat = lambda a: a.reshape(ways, -1)
    vectors = jnp.concatenate(
        [
            flat(grad_attn_gain), flat(grad_attn_shift), flat(grad_ffn_gain),
            flat(grad_ffn_shift), flat(grad_down_bias), flat(grad_up_bias), flat(grad_rel_table),
        ],
        axis=1,
    )
    activ_next = after(activ, grad_tokens)
    if by_pieces:
        high_parts = third(after_all(high_parts, grad_tokens))
        low_parts = along_one(after_all(low_parts, grad_tokens))
        activ_next = after(activ_next, low_parts[0], high_parts[0])
    sum_down, sum_up = widen(total(after(share_ffn, low_sent)))
    output = output_of(start, activ_next, down_full, middle, down_bias_full)
    if by_pieces:
        for bit in (1, 2, 4):
            vectors = vectors + swap(vectors, bit)
        mine = lax.dynamic_slice_in_dim(vectors, lax.axis_index("fsdp"), 1, 0)
        for bit in (1, 2):
            mine = mine + swap_rep(mine, bit)
        low_parts = along_two(after_all(low_parts, output))
        high_parts = along_one(after_all(high_parts, output))
        low_own = quarter_sum(*low_parts)
        high_parts = along_two(after_all(high_parts, sum_down, sum_up))
        low_next = swap_rep(low_own, 2)
        high_own = quarter_sum(*high_parts)
        high_next = swap_rep(high_own, 2)
        low_far = swap_rep(jnp.concatenate([low_own, low_next], axis=0), 1)
        high_far = swap_rep(jnp.concatenate([high_own, high_next], axis=0), 1)
        sum_qkv, sum_out = spread(
            place, low_own, low_next, low_far, high_own, high_next, high_far
        )
    else:
        mine = total(scatter(vectors))
        sum_out = total(share_out)
        sum_qkv = jnp.stack(
            [total(share_low).reshape(-1, 3, 512), total(share_high).reshape(-1, 3, 512)], axis=2
        ).reshape(-1, 3 * D)
    cut = lambda i: mine[0, cuts[i] : cuts[i + 1]]
    return (
        output, grad_tokens, cut(0), cut(1), sum_qkv.astype(f32), cut(6).reshape(-1, H),
        sum_out.astype(f32), cut(2), cut(3), sum_up, cut(5),
        sum_down, cut(4),
    )


def solution(mesh):
    rows, vec, mat = P(("rep", "fsdp"), None), P("fsdp"), P("fsdp", None)
    in_specs = (rows, rows, vec, vec, mat, mat, mat, vec, vec, mat, vec, mat, vec, rows)
    out_specs = (rows, rows, vec, vec, mat, mat, mat, vec, vec, mat, vec, mat, vec)
    return jax.shard_map(local, mesh=mesh, in_specs=in_specs, out_specs=out_specs, check_vma=False)
```

```python
import functools

import jax
import jax.numpy as jnp
import numpy as np
from jax import lax
from jax.experimental import pallas as pl
from jax.experimental.pallas import tpu as pltpu
from jax.sharding import PartitionSpec as P

D = 1024
H = 16
HD = 64
FF = 4096
NBUCKET = 32
MAXDIST = 128
bf16 = jnp.bfloat16
f32 = jnp.float32
NEG = -1e9
LONG = 1024
SHORT = 256
T = 1280
NN = (((1,), (0,)), ((), ()))
NT = (((1,), (1,)), ((), ()))
TN = (((0,), (0,)), ((), ()))


def dot(a, b, dims):
    return lax.dot_general(a, b, dims, preferred_element_type=f32)


def split3(x):
    a = x.astype(bf16)
    r = x - a.astype(f32)
    b = r.astype(bf16)
    return a, b, (r - b.astype(f32)).astype(bf16)


def near_band(g):
    r = lax.broadcasted_iota(jnp.int32, (128, 256), 0)
    c = lax.broadcasted_iota(jnp.int32, (128, 256), 1)
    return jnp.where(c < r, NEG, pltpu.roll(jnp.broadcast_to(g, (128, 256)), 0, 1, stride=1, stride_axis=0))


def fwd_body(bnd_ref, g_ref, q_ref, k_ref, v_ref, o_ref, qa_ref):
    lane = lax.broadcasted_iota(jnp.int32, (1, 128), 1)
    bnd = bnd_ref[0]
    bands = [near_band(g_ref[0, h : h + 1, :]) for h in range(2)]
    for blk in range(5):
        R = 256 * blk
        lo = 0 if blk < 4 else 1024
        nk = R + 256 - lo
        qrow = q_ref[R : R + 256, :] * bf16(0.125)
        outs = []
        for h in range(2):
            mine = (lane < 64) if h == 0 else (lane >= 64)
            band = bands[h]

            def visible(x, key, query):
                if blk < 4:
                    return x
                rr = lax.broadcasted_iota(jnp.int32, x.shape, 0) + key
                cc = lax.broadcasted_iota(jnp.int32, x.shape, 1) + query
                return jnp.where((cc >= bnd) & (rr < bnd), NEG, x)

            st = dot(k_ref[lo : R + 256, :], jnp.where(mine, qrow, bf16(0)), NT)
            pieces = []
            if nk > 384:
                pieces.append(st[: nk - 384])
            if nk > 256:
                edge = st[nk - 384 : nk - 256]
                pieces.append(
                    jnp.concatenate([edge[:, :128] + band[:, 128:], edge[:, 128:]], axis=1)
                )
            pieces.append(visible(st[nk - 256 : nk - 128] + band, 0, 0))
            last = visible(st[nk - 128 :, 128:] + band[:, :128], 128, 128)
            top = None
            for piece in pieces:
                m = jnp.max(piece, axis=0, keepdims=True)
                top = m if top is None else jnp.maximum(top, m)
            right = jnp.maximum(top[:, 128:], jnp.max(last, axis=0, keepdims=True))
            top = jnp.concatenate([top[:, :128], right], axis=1)
            probs = [jnp.exp(piece - top).astype(bf16) for piece in pieces]
            probs.append(
                jnp.concatenate(
                    [jnp.zeros((128, 128), bf16), jnp.exp(last - right).astype(bf16)], axis=1
                )
            )
            va = jnp.where(mine, v_ref[lo : R + 256, :], bf16(1))
            o = dot(jnp.concatenate(probs, axis=0), va, TN)
            outs.append(o)
            lse = jnp.transpose(jnp.broadcast_to(top, (128, 256))) + jnp.log(
                jnp.where(mine, 1.0, o)
            )
            a, b, c = split3(lse)
            base = 64 if h == 0 else 0
            qa_ref[R : R + 256, 128 * h : 128 * h + 128] = jnp.where(
                mine, qrow,
                jnp.where(lane == base, a, jnp.where(lane == base + 1, b, jnp.where(lane == base + 2, c, bf16(0)))),
            )
        total = pltpu.roll(jnp.where(lane < 64, outs[1], outs[0]), 64, 1)
        o_ref[R : R + 256, :] = (jnp.where(lane < 64, outs[0], outs[1]) / total).astype(bf16)

def attn_fwd(packed,g,bnd):
    return pl.pallas_call(fwd_body,
        grid=(8,),
        in_specs=[pl.BlockSpec(memory_space=pltpu.SMEM),
                  pl.BlockSpec((1,2,256),lambda i:(i,0,0)),
                  pl.BlockSpec((T,128),lambda i:(0,i)),
                  pl.BlockSpec((T,128),lambda i:(0,8+i)),
                  pl.BlockSpec((T,128),lambda i:(0,16+i))],
        out_specs=[pl.BlockSpec((T,128),lambda i:(0,i)),pl.BlockSpec((T,256),lambda i:(0,i))],
        out_shape=[jax.ShapeDtypeStruct((T,1024),bf16),jax.ShapeDtypeStruct((T,2048),bf16)],
        cost_estimate=cost(27),
        compiler_params=pltpu.CompilerParams(vmem_limit_bytes=48<<20))(bnd,g,packed,packed,packed)

def bwd_body(bnd_ref,g_ref,qa_ref,k_ref,v_ref,o_ref,do_ref,grad_ref,gs_ref,dq_acc,band_acc):
    lane=lax.broadcasted_iota(jnp.int32,(1,128),1)
    bnd=bnd_ref[0]
    r1=lax.broadcasted_iota(jnp.int32,(128,256),0); c1=lax.broadcasted_iota(jnp.int32,(128,256),1)
    prod=do_ref[...].astype(f32)*o_ref[...].astype(f32)
    ph=prod.astype(bf16); plo=(prod-ph.astype(f32)).astype(bf16)
    i0=lax.broadcasted_iota(jnp.int32,(128,128),0); j0=lax.broadcasted_iota(jnp.int32,(128,128),1)
    sw=jnp.where((i0<64)!=(j0<64),bf16(1),bf16(0))
    delta=-(dot(ph,sw,NN)+dot(plo,sw,NN))
    dh,dl,_=split3(delta)
    gks=[];gvs=[]
    for h in range(2):
        mine=(lane<64) if h==0 else (lane>=64)
        base=64 if h==0 else 0
        g=g_ref[0,h:h+1,:]
        band=pltpu.roll(jnp.broadcast_to(g,(128,256)),0,1,stride=1,stride_axis=0)
        band=jnp.where(c1<r1,NEG,band)
        dob=do_ref[...]
        doa=jnp.where(mine,dob,jnp.where(lane==base,dh,jnp.where(lane==base+1,dl,bf16(0))))
        gk=[];gv=[]
        for blk in (3,2,1,0,4):
            R=256*blk
            hi=1024 if blk<4 else 1280
            nq=hi-R
            neg=jnp.where((lane>=base)&(lane<base+3),bf16(-1),bf16(0))
            one=jnp.where((lane>=base)&(lane<base+2),bf16(1),bf16(0))
            ka=jnp.where(mine,k_ref[R:R+256,:],neg)
            va=jnp.where(mine,v_ref[R:R+256,:],one)
            qa=qa_ref[R:hi,128*h:128*h+128]
            do=doa[R:hi]
            st=dot(ka,qa,NT)
            dpt=dot(va,do,NT)
            pr=[];dr=[]
            for sub in range(2):
                b0=128*sub
                w=min(256,nq-b0)
                sb=st[b0:b0+128,b0:b0+w]+band[:,:w]
                if blk==4:
                    rr=lax.broadcasted_iota(jnp.int32,sb.shape,0)+b0
                    cc=lax.broadcasted_iota(jnp.int32,sb.shape,1)+b0
                    sb=jnp.where((cc>=bnd)&(rr<bnd),NEG,sb)
                pb=jnp.exp(sb)
                db=pb*dpt[b0:b0+128,b0:b0+w]
                if h==0 or True:
                    if blk==3 and sub==0: band_acc[...]=db
                    elif w==256: band_acc[...]+=db
                    else: band_acc[:,:w]+=db
                ps=[pb.astype(bf16)]; ds=[db.astype(bf16)]
                if sub==1:
                    ps.insert(0,jnp.zeros((128,128),bf16)); ds.insert(0,jnp.zeros((128,128),bf16))
                if b0+w<nq:
                    pf=jnp.exp(st[b0:b0+128,b0+w:])
                    df=pf*dpt[b0:b0+128,b0+w:]
                    ps.append(pf.astype(bf16)); ds.append(df.astype(bf16))
                pr.append(jnp.concatenate(ps,axis=1) if len(ps)>1 else ps[0])
                dr.append(jnp.concatenate(ds,axis=1) if len(ds)>1 else ds[0])
            p=jnp.concatenate(pr,axis=0); ds=jnp.concatenate(dr,axis=0)
            gvb=dot(p,do,NN); gkb=dot(ds,qa,NN)
            dqb=dot(ds,ka,TN)
            if blk in (3,2,1,0):
                dq_acc[h,R:R+256,:]=dqb[:256]
                if nq>256: dq_acc[h,R+256:hi,:]+=dqb[256:]
            else:
                dq_acc[h,R:hi,:]=dqb
            gk.append((R,gkb)); gv.append((R,gvb))
        gks.append(gk);gvs.append(gv)
        Y=band_acc[...]
        n=64
        while n>=1:
            Y=Y[:n]+pltpu.roll(Y[n:2*n],256-n,1)
            n//=2
        gs_ref[0,h:h+1,:]=Y
    for (R,a),(_,b) in zip(*gks): grad_ref[1,R:R+256,:]=jnp.where(lane<64,a,b).astype(bf16)
    for (R,a),(_,b) in zip(*gvs): grad_ref[2,R:R+256,:]=jnp.where(lane<64,a,b).astype(bf16)
    grad_ref[0]=(jnp.where(lane<64,dq_acc[0],dq_acc[1])*0.125).astype(bf16)

def attn_bwd(packed,qa,o,do,g,bnd,half):
    sp=lambda off: pl.BlockSpec((T,128),lambda i:(0,off+4*half+i))
    return pl.pallas_call(bwd_body,
        grid=(4,),
        in_specs=[pl.BlockSpec(memory_space=pltpu.SMEM),
                  pl.BlockSpec((1,2,256),lambda i:(4*half+i,0,0)),
                  pl.BlockSpec((T,256),lambda i:(0,4*half+i)),sp(8),sp(16),sp(0),sp(0)],
        out_specs=[pl.BlockSpec((3,T,128),lambda i:(0,0,i)),pl.BlockSpec((1,2,256),lambda i:(i,0,0))],
        out_shape=[jax.ShapeDtypeStruct((3,T,512),bf16),jax.ShapeDtypeStruct((4,2,256),f32)],
        scratch_shapes=[pltpu.VMEM((2,T,128),f32),pltpu.VMEM((128,256),f32)],
        cost_estimate=cost(22.5),
        compiler_params=pltpu.CompilerParams(vmem_limit_bytes=56<<20))(bnd,g,qa,packed,packed,o,do)


def shape(*dims, dtype=bf16):
    return jax.ShapeDtypeStruct(dims, dtype)


def whole(*dims):
    return pl.BlockSpec(dims, lambda i: (0,) * len(dims))


def columns(rows, width, first=0):
    return pl.BlockSpec((rows, width), lambda i: (0, first + i))


SCALAR = pl.BlockSpec(memory_space=pltpu.SMEM)


def cost(us):
    return pl.CostEstimate(flops=int(us * 1.15e9), bytes_accessed=0, transcendentals=0)


def call(body, grid, in_specs, out_specs, out_shape, scratch=(), us=1.0, aliases={}):
    return pl.pallas_call(
        body,
        grid=(grid,),
        in_specs=in_specs,
        out_specs=out_specs,
        out_shape=out_shape,
        scratch_shapes=list(scratch),
        input_output_aliases=aliases,
        cost_estimate=cost(us),
        compiler_params=pltpu.CompilerParams(vmem_limit_bytes=58 << 20),
    )


def row_stats(x):
    mean = jnp.mean(x, axis=-1, keepdims=True)
    center = x - mean
    rstd = lax.rsqrt(jnp.mean(center * center, axis=-1, keepdims=True) + 1e-05)
    return center * rstd, rstd


def back_through_norm(xhat, rstd, scaled):
    return rstd * (
        scaled
        - jnp.mean(scaled, axis=-1, keepdims=True)
        - xhat * jnp.mean(scaled * xhat, axis=-1, keepdims=True)
    )


def shifted_rows(ext, offset, r):
    fine = lax.rem(offset, 8)
    rows = ext[pl.ds(pl.multiple_of(offset - fine + r, 8), 136), :].reshape(17, 8, D)
    rows = pltpu.roll(rows, lax.rem(8 - fine, 8), 1)
    keep = lax.broadcasted_iota(jnp.int32, (1, 8, D), 1) < 8 - fine
    return jnp.where(keep, rows[:16], rows[1:]).reshape(128, D)


def prep_body(start_ref, tok_ref, cot_ref, tok_out, cot_out, bias_out, ext):
    start = start_ref[0]
    for source, target in ((tok_ref, tok_out), (cot_ref, cot_out)):
        for r in range(0, T, 256):
            ext[r : r + 256, :] = source[r : r + 256, :].astype(f32)
        ext[T : T + SHORT, :] = source[0:SHORT, :].astype(f32)
        total = None
        for r in range(0, T, 128):
            rows = shifted_rows(ext, start, r)
            target[r : r + 128, :] = rows.astype(bf16)
            if target is cot_out:
                part = jnp.sum(rows, axis=0, keepdims=True)
                total = part if total is None else total + part
    bias_out[...] = total


def prep(start, tokens, cotangent):
    return call(
        prep_body, 1,
        [SCALAR, whole(T, D), whole(T, D)],
        [whole(T, D), whole(T, D), whole(1, D)],
        [shape(T, D), shape(T, D), shape(1, D, dtype=f32)],
        [pltpu.VMEM((T + SHORT + 8, D), f32)],
        us=7,
    )(start, tokens, cotangent)


def qkv_body(tok_ref, gain_ref, shift_ref, w_ref, packed_ref, normed_ref):
    @pl.when(pl.program_id(0) == 0)
    def _():
        for r in range(0, T, 256):
            xhat, _ = row_stats(tok_ref[r : r + 256, :].astype(f32))
            normed_ref[r : r + 256, :] = (xhat * gain_ref[...] + shift_ref[...]).astype(bf16)

    packed_ref[...] = dot(normed_ref[...], w_ref[...], NN).astype(bf16)


def qkv_forward(tok, gain, shift, w_qkv):
    return call(
        qkv_body, 6,
        [whole(T, D), whole(1, D), whole(1, D), columns(D, 512)],
        [columns(T, 512), whole(T, D)],
        [shape(T, 3 * D), shape(T, D)],
        us=15,
    )(tok, gain, shift, w_qkv)


PIECES = (
    (0, 0, 128), (1, 0, 128), (2, 0, 128), (4, 0, 128), (6, 0, 64), (6, 64, 64),
    (3, 0, 128), (5, 0, 128), (7, 0, 64), (7, 64, 64),
)


def qkv_pieces_body(me_ref, tok_ref, gain_ref, shift_ref, *refs):
    pieces = refs[: len(PIECES)]
    packed_ref, normed_ref, w_out, w_all, arrived, left = refs[len(PIECES) :]
    step = pl.program_id(0)
    save = pltpu.make_async_copy(w_all, w_out, left)

    @pl.when(step == 0)
    def _():
        copies = []
        for n, (other, first, rows) in enumerate(PIECES):
            at = pl.multiple_of((me_ref[0] ^ other) * 128 + first, 64)
            copy = pltpu.make_async_copy(pieces[n], w_all.at[pl.ds(at, rows), :], arrived.at[n])
            copy.start()
            copies.append(copy)
        for r in range(0, T, 256):
            xhat, _ = row_stats(tok_ref[r : r + 256, :].astype(f32))
            normed_ref[r : r + 256, :] = (xhat * gain_ref[...] + shift_ref[...]).astype(bf16)
        for copy in copies:
            copy.wait()
        save.start()

    at = pl.multiple_of(step * 512, 512)
    packed_ref[...] = dot(normed_ref[...], w_all[:, pl.ds(at, 512)], NN).astype(bf16)

    @pl.when(step == pl.num_programs(0) - 1)
    def _():
        save.wait()


def qkv_forward_pieces(me, tok, gain, shift, pieces):
    anywhere = pl.BlockSpec(memory_space=pl.ANY)
    return call(
        qkv_pieces_body, 6,
        [SCALAR, whole(T, D), whole(1, D), whole(1, D)] + [anywhere] * len(PIECES),
        [columns(T, 512), whole(T, D), anywhere],
        [shape(T, 3 * D), shape(T, D), shape(D, 3 * D)],
        [
            pltpu.VMEM((D, 3 * D), bf16),
            pltpu.SemaphoreType.DMA((len(PIECES),)),
            pltpu.SemaphoreType.DMA,
        ],
        us=16,
    )(me, tok, gain, shift, *pieces)


def out_body(mixed_ref, w_ref, tok_ref, gain_ref, shift_ref, middle_ref, normed_ref):
    middle = tok_ref[...].astype(f32) + dot(mixed_ref[...], w_ref[...], NN)
    middle_ref[...] = middle.astype(bf16)
    xhat, _ = row_stats(middle)
    normed_ref[...] = (xhat * gain_ref[...] + shift_ref[...]).astype(bf16)


def out_forward(mixed, w_out_up, tok, gain, shift):
    rows = pl.BlockSpec((256, D), lambda i: (i, 0))
    return call(
        out_body, T // 256,
        [rows, whole(D, D), rows, whole(1, D), whole(1, D)],
        [rows, rows],
        [shape(T, D), shape(T, D)],
        us=8.6,
    )(mixed, w_out_up, tok, gain, shift)


C0 = float(np.sqrt(2.0 / np.pi))
C1 = 0.044715 * C0


def up_body(normed_ref, w_ref, bias_ref, activ_ref, slope_ref, *held):
    chunks = [(r, c) for c in range(0, 512, 256) for r in range(0, T, 128)]

    def finish(n, later):
        r, c = chunks[n]
        bias = bias_ref[:, c : c + 256]
        if later is not None:
            bias = bias + 0.0 * held[later % 6][120:121, :]
        for q in range(0, 128, 16):
            u = held[n % 6][q : q + 16, :] + bias
            square = u * u
            half = 0.5 * jnp.tanh(u * (C0 + C1 * square)) + 0.5
            activ = u * half
            activ_ref[r + q : r + q + 16, c : c + 256] = activ.astype(bf16)
            slope = half + activ * (1.0 - half) * (2.0 * C0 + 6.0 * C1 * square)
            slope_ref[r + q : r + q + 16, c : c + 256] = slope.astype(bf16)

    for n, (r, c) in enumerate(chunks):
        held[n % 6][...] = dot(normed_ref[r : r + 128, :], w_ref[:, c : c + 256], NN)
        if n >= 2:
            finish(n - 2, n - 1)
    finish(len(chunks) - 2, None)
    finish(len(chunks) - 1, None)


def up_forward(normed_two, w_out_up, up_bias):
    return call(
        up_body, 8,
        [whole(T, D), columns(D, 512, 2), columns(1, 512)],
        [columns(T, 512), columns(T, 512)],
        [shape(T, FF), shape(T, FF)],
        [pltpu.VMEM((128, 256), f32)] * 6,
        us=21.3,
    )(normed_two, w_out_up, up_bias)


def grad_down_body(activ_ref, cot_ref, out_ref):
    out_ref[0, 0] = dot(activ_ref[...], cot_ref[...], TN).astype(bf16).reshape(out_ref.shape[2:])


def ffn_shape(ways):
    return shape(ways, 2, 4, D // ways, D)


def grad_down(activ, cot, ways):
    rows = FF // ways
    return call(
        grad_down_body, ways,
        [columns(T, rows), whole(T, D)],
        pl.BlockSpec((1, 1, 4, D // ways, D), lambda i: (i, 0, 0, 0, 0)),
        ffn_shape(ways),
        us=16.3,
    )(activ, cot)


def grad_up_body(left_ref, right_ref, held_ref, out_ref):
    value = dot(left_ref[...], right_ref[...], TN).astype(bf16)
    out_ref[...] = value.reshape(out_ref.shape)


def grad_up(left, right, held, ways):
    return call(
        grad_up_body, 8,
        [whole(T, D), columns(T, 512), pl.BlockSpec(memory_space=pl.ANY)],
        pl.BlockSpec((ways, 1, 1, D // ways, 512), lambda i: (0, 1, i // 2, 0, i % 2)),
        ffn_shape(ways),
        us=16.3, aliases={2: 0},
    )(left, right, held)


def grad_pre_body(cot_ref, w_ref, slope_ref, pre_ref, bias_ref):
    total = None
    for r in range(0, T, 256):
        pre = (
            dot(cot_ref[r : r + 256, :], w_ref[...], NT) * slope_ref[r : r + 256, :].astype(f32)
        ).astype(bf16)
        pre_ref[r : r + 256, :] = pre
        part = jnp.sum(pre.astype(f32), axis=0, keepdims=True)
        total = part if total is None else total + part
    bias_ref[...] = total


def grad_pre_of(cot, w_down, slope):
    return call(
        grad_pre_body, 8,
        [whole(T, D), pl.BlockSpec((512, D), lambda i: (i, 0)), columns(T, 512)],
        [columns(T, 512), columns(1, 512)],
        [shape(T, FF), shape(1, FF, dtype=f32)],
        us=19,
    )(cot, w_down, slope)


def grad_tile_body(left_ref, right_ref, out_ref):
    right = right_ref[...]
    right = right.reshape(right.shape[-2:])
    out_ref[...] = dot(left_ref[...], right, TN).astype(bf16)


def right_tiles(right):
    if right.ndim == 3:
        return right.shape[0], pl.BlockSpec((1, T, 512), lambda i: (i, 0, 0))
    return right.shape[1] // 512, columns(T, 512)


def grad_columns(left, right):
    tiles, spec = right_tiles(right)
    return call(
        grad_tile_body, tiles,
        [whole(T, D), spec],
        columns(D, 512),
        shape(D, tiles * 512),
        us=2.0 * tiles,
    )(left, right)


def take_blocks(me, left_ref, held):
    for n in range(8):
        core = (me & 1) if n >= 4 else 1 - (me & 1)
        at = pl.multiple_of((((me >> 1) ^ (n % 4)) * 2 + core) * 128, 128)
        held[:, 128 * n : 128 * n + 128] = left_ref[:, pl.ds(at, 128)]


def grad_blocks(me, lefts, rights):
    specs, begins, first = [SCALAR], [], 0
    for right in rights:
        if right.ndim == 3:
            count = right.shape[0]
            spec = pl.BlockSpec(
                (1, T, 512), lambda i, a=first, n=count: (jnp.clip(i - a, 0, n - 1), 0, 0)
            )
        else:
            count = right.shape[1] // 512
            spec = pl.BlockSpec(
                (T, 512), lambda i, a=first, n=count: (0, jnp.clip(i - a, 0, n - 1))
            )
        specs.append(spec)
        begins.append(first)
        first += count
    n, tiles = len(lefts), first

    def body(me_ref, *refs):
        theirs, mine, held = refs[2 * n :]
        step = pl.program_id(0)
        for begin, end, left_ref, right_ref in zip(
            begins, begins[1:] + [tiles], refs[n : 2 * n], refs[:n]
        ):

            @pl.when(step == begin)
            def _():
                take_blocks(me_ref[0], left_ref, held)

            @pl.when((step >= begin) & (step < end))
            def _():
                right = right_ref[...]
                value = dot(held[...], right.reshape(right.shape[-2:]), TN).astype(bf16)
                theirs[...] = value[:512]
                mine[...] = value[512:]

    return call(
        body, tiles, specs + [whole(T, D)] * n, [columns(512, 512)] * 2,
        [shape(512, tiles * 512)] * 2,
        [pltpu.VMEM((T, D), bf16)],
        us=1.5 + 2.3 * tiles,
    )(me, *rights, *lefts)


def core_sum_body(mine, other, a_send, a_keep, b_send, b_keep):
    for rel, a, b, place_a, place_b in (
        (0, a_keep, b_keep, 0, 0), (1, a_send, b_keep, 0, 1),
        (2, a_keep, b_send, 1, 0), (3, a_send, b_send, 1, 1),
    ):
        rows = slice(128 * rel, 128 * rel + 128)
        total = (mine[rows, :].astype(f32) + other[rows, :].astype(f32)).astype(bf16)
        a[place_a] = total[:, :256]
        b[place_b] = total[:, 256:]


def core_sum(mine, other):
    tiles = mine.shape[1] // 512
    part = pl.BlockSpec((2, 128, 256), lambda i: (0, 0, i))
    return call(
        core_sum_body, tiles, [columns(512, 512)] * 2, [part] * 4,
        [shape(2, 128, tiles * 256)] * 4,
        us=0.1,
    )(mine, other)


def pair_sum_body(a_keep, a_got, b_keep, b_got, a_send, a_rest, b_send, b_rest):
    for keep, got, send, rest in ((a_keep, a_got, a_send, a_rest), (b_keep, b_got, b_send, b_rest)):
        for place, target in ((1, send), (0, rest)):
            target[...] = (keep[place].astype(f32) + got[place].astype(f32)).astype(bf16)


def pair_sum(*parts):
    width = parts[0].shape[2]
    return call(
        pair_sum_body, 1,
        [whole(2, 128, width)] * 4,
        [whole(128, width)] * 4,
        [shape(128, width)] * 4,
        us=0.1,
    )(*parts)


def add(a_ref, b_ref):
    return a_ref[...].astype(f32) + b_ref[...].astype(f32)


def last_sum_body(place_ref, small, *refs):
    *parts, send, keep = refs
    bit = place_ref[0] & 1
    first = 0
    for n in range(0, len(parts), 4):
        for lane, (one, two) in enumerate((parts[n : n + 2], parts[n + 2 : n + 4])):
            for target, mine in ((keep, bit), (send, 1 - bit)):
                at = pl.ds(pl.multiple_of(mine * 64, 64), 64)
                total = (one[at, :].astype(f32) + two[at, :].astype(f32)).astype(bf16)
                for tile in range(total.shape[1] // 256):
                    to = first + 512 * tile + 256 * lane
                    target[:, to : to + 256] = total[:, 256 * tile : 256 * tile + 256]
        first += 2 * parts[n].shape[1]
    for target, mine in ((keep, bit), (send, 1 - bit)):
        target[:, first:] = small[pl.ds(pl.multiple_of(mine * 64, 64), 64), :]


def last_sum(place, small, *parts):
    width = sum(part.shape[1] for part in parts) // 2 + small.shape[1]
    return call(
        last_sum_body, 1,
        [SCALAR] + [whole(*part.shape) for part in (small,) + parts],
        [whole(64, width)] * 2,
        [shape(64, width)] * 2,
        us=0.1,
    )(place, small, *parts)


def half_sum_body(place_ref, keep, got, send, rest):
    bit = place_ref[0] >> 1
    rows = send.shape[0]
    for target, mine in ((rest, bit), (send, 1 - bit)):
        at = pl.ds(pl.multiple_of(mine * rows, rows), rows)
        target[...] = (keep[at, :].astype(f32) + got[at, :].astype(f32)).astype(bf16)


def half_sum(place, keep, got):
    rows, width = keep.shape
    return call(
        half_sum_body, 1,
        [SCALAR] + [whole(rows, width)] * 2,
        [whole(rows // 2, width)] * 2,
        [shape(rows // 2, width)] * 2,
        us=0.1,
    )(place, keep, got)


def quarter_sum_body(keep, got, out):
    out[...] = (keep[...].astype(f32) + got[...].astype(f32)).astype(bf16)


def quarter_sum(keep, got):
    return call(
        quarter_sum_body, 1, [whole(*keep.shape)] * 2, whole(*keep.shape), shape(*keep.shape),
        us=0.1,
    )(keep, got)


def quarters(place_ref, own, near, far):
    one, two, rows = place_ref[0] & 1, place_ref[0] >> 1, own.shape[0]
    for ref, cut, bit_one, bit_two in (
        (own, slice(0, rows), one, two),
        (near, slice(0, rows), one, 1 - two),
        (far, slice(0, rows), 1 - one, two),
        (far, slice(rows, 2 * rows), 1 - one, 1 - two),
    ):
        yield ref, cut, pl.ds(pl.multiple_of((bit_one * 2 + bit_two) * rows, rows), rows)


def spread_body(place_ref, own, near, far, qkv_out, out_out, small_out):
    for ref, cut, at in quarters(place_ref, own, near, far):
        for half, start in ((0, 0), (1, 2560)):
            for n in range(3):
                to = 1024 * n + 512 * half
                qkv_out[at, to : to + 512] = ref[
                    cut, start + 512 * n : start + 512 * n + 512
                ].astype(f32)
        out_out[at, :] = ref[cut, 1536:2560].astype(f32)
        small_out[at, :] = ref[cut, 4 * D :].astype(f32)


def spread(place, *parts):
    return call(
        spread_body, 1,
        [SCALAR] + [whole(*part.shape) for part in parts],
        [whole(128, 3 * D), whole(128, D), whole(128, 128)],
        [shape(128, 3 * D, dtype=f32), shape(128, D, dtype=f32), shape(128, 128, dtype=f32)],
        us=0.1,
    )(place, *parts)


def widen_body(sum_ref, down_ref, up_ref):
    rows = sum_ref.shape[3]
    for k in range(4):
        down_ref[rows * k : rows * k + rows, :] = sum_ref[0, 0, k].astype(f32)
        up_ref[:, D * k : D * k + D] = sum_ref[0, 1, k].astype(f32)


def widen(total):
    rows = total.shape[3]
    return call(
        widen_body, 1,
        [whole(*total.shape)],
        [whole(4 * rows, D), whole(rows, FF)],
        [shape(4 * rows, D, dtype=f32), shape(rows, FF, dtype=f32)],
        us=0.1,
    )(total)


ANYWHERE = pl.BlockSpec(memory_space=pl.ANY)


def fetch(pairs, sems):
    return [pltpu.make_async_copy(one, two, sems.at[n]) for n, (one, two) in enumerate(pairs)]


def mid_body(
    pre_ref, up_ref, middle_any, cot_any, gain_ref, out_up_any,
    att_any, mixed_any, gain_out, shift_out, acc, middle, cot, w_out, att, mixed, got, put,
):
    step = pl.program_id(0)
    loads = fetch(
        ((middle_any, middle), (cot_any, cot), (out_up_any.at[:, pl.ds(0, D)], w_out)), got
    )

    @pl.when(step == 0)
    def _():
        for load in loads:
            load.start()
        acc[...] = dot(pre_ref[...], up_ref[...], NT)

    @pl.when(step > 0)
    def _():
        acc[...] += dot(pre_ref[...], up_ref[...], NT)

    @pl.when(step == pl.num_programs(0) - 1)
    def _():
        for load in loads:
            load.wait()
        gains = shifts = None
        stores = []
        for n, r in enumerate(range(0, T, 256)):
            rows = slice(r, r + 256)
            g = acc[rows, :]
            xhat, rstd = row_stats(middle[rows, :].astype(f32))
            a = jnp.sum(g * xhat, axis=0, keepdims=True)
            b = jnp.sum(g, axis=0, keepdims=True)
            gains = a if gains is None else gains + a
            shifts = b if shifts is None else shifts + b
            mid = cot[rows, :].astype(f32) + back_through_norm(xhat, rstd, g * gain_ref[...])
            att[rows, :] = mid.astype(bf16)
            mixed[rows, :] = dot(att[rows, :], w_out[...], NT).astype(bf16)
            for one, two, sem in ((att, att_any, 2 * n), (mixed, mixed_any, 2 * n + 1)):
                store = pltpu.make_async_copy(
                    one.at[pl.ds(r, 256), :], two.at[pl.ds(r, 256), :], put.at[sem]
                )
                store.start()
                stores.append(store)
        gain_out[...] = gains
        shift_out[...] = shifts
        for store in stores:
            store.wait()


def grad_middle_of(grad_pre, w_out_up, middle, cot, gain):
    return call(
        mid_body, 8,
        [columns(T, 512), columns(D, 512, 2), ANYWHERE, ANYWHERE, whole(1, D), ANYWHERE],
        [ANYWHERE, ANYWHERE, whole(1, D), whole(1, D)],
        [shape(T, D), shape(T, D), shape(1, D, dtype=f32), shape(1, D, dtype=f32)],
        [
            pltpu.VMEM((T, D), f32), pltpu.VMEM((T, D), bf16), pltpu.VMEM((T, D), bf16),
            pltpu.VMEM((D, D), bf16), pltpu.VMEM((T, D), bf16), pltpu.VMEM((T, D), bf16),
            pltpu.SemaphoreType.DMA((3,)), pltpu.SemaphoreType.DMA((10,)),
        ],
        us=23.5,
    )(grad_pre, w_out_up, middle, cot, gain, w_out_up)


def unrotate(ext, start, staged, out_any, sems):
    ext[0:SHORT, :] = ext[T : T + SHORT, :]
    stores = []
    for n, r in enumerate(range(0, T, 128)):
        staged[r : r + 128, :] = shifted_rows(ext, SHORT - start, r).astype(bf16)
        store = pltpu.make_async_copy(
            staged.at[pl.ds(r, 128), :], out_any.at[pl.ds(r, 128), :], sems.at[n]
        )
        store.start()
        stores.append(store)
    for store in stores:
        store.wait()


def tok_body(
    start_ref, low_ref, high_ref, w_ref, tok_any, mid_any, gain_ref,
    grad_any, gain_out, shift_out, ext, tok, mid, staged, got, put,
):
    step = pl.program_id(0)
    loads = fetch(((tok_any, tok), (mid_any, mid)), got)

    @pl.when(step == 0)
    def _():
        for load in loads:
            load.start()
        ext[SHORT : SHORT + T, :] = dot(low_ref[0], w_ref[...], NT)

    @pl.when((step > 0) & (lax.rem(step, 2) == 0))
    def _():
        ext[SHORT : SHORT + T, :] += dot(low_ref[0], w_ref[...], NT)

    @pl.when(lax.rem(step, 2) == 1)
    def _():
        ext[SHORT : SHORT + T, :] += dot(high_ref[0], w_ref[...], NT)

    @pl.when(step == pl.num_programs(0) - 1)
    def _():
        for load in loads:
            load.wait()
        gains = shifts = None
        for r in range(0, T, 256):
            g = ext[SHORT + r : SHORT + r + 256, :]
            xhat, rstd = row_stats(tok[r : r + 256, :].astype(f32))
            a = jnp.sum(g * xhat, axis=0, keepdims=True)
            b = jnp.sum(g, axis=0, keepdims=True)
            gains = a if gains is None else gains + a
            shifts = b if shifts is None else shifts + b
            ext[SHORT + r : SHORT + r + 256, :] = mid[r : r + 256, :].astype(f32) + (
                back_through_norm(xhat, rstd, g * gain_ref[...])
            )
        gain_out[...] = gains
        shift_out[...] = shifts
        unrotate(ext, start_ref[0], staged, grad_any, put)


def grad_tokens_of(start, low, high, w_qkv, tok, mid, gain):
    half = pl.BlockSpec((1, T, 512), lambda i: (i // 2, 0, 0))
    return call(
        tok_body, 6,
        [SCALAR, half, half, columns(D, 512), ANYWHERE, ANYWHERE, whole(1, D)],
        [ANYWHERE, whole(1, D), whole(1, D)],
        [shape(T, D), shape(1, D, dtype=f32), shape(1, D, dtype=f32)],
        [
            pltpu.VMEM((T + SHORT + 8, D), f32), pltpu.VMEM((T, D), bf16),
            pltpu.VMEM((T, D), bf16), pltpu.VMEM((T, D), bf16),
            pltpu.SemaphoreType.DMA((2,)), pltpu.SemaphoreType.DMA((10,)),
        ],
        us=0.1,
    )(start, low, high, w_qkv, tok, mid, gain)


def output_body(
    start_ref, activ_ref, w_ref, middle_any, bias_ref, out_any, ext, middle, staged, got, put
):
    step = pl.program_id(0)
    loads = fetch(((middle_any, middle),), got)

    @pl.when(step == 0)
    def _():
        loads[0].start()
        ext[SHORT : SHORT + T, :] = dot(activ_ref[...], w_ref[...], NN)

    @pl.when(step > 0)
    def _():
        ext[SHORT : SHORT + T, :] += dot(activ_ref[...], w_ref[...], NN)

    @pl.when(step == pl.num_programs(0) - 1)
    def _():
        loads[0].wait()
        for r in range(0, T, 256):
            ext[SHORT + r : SHORT + r + 256, :] += (
                middle[r : r + 256, :].astype(f32) + bias_ref[...]
            )
        unrotate(ext, start_ref[0], staged, out_any, put)


def output_of(start, activ, w_down, middle, bias):
    return call(
        output_body, 8,
        [SCALAR, columns(T, 512), pl.BlockSpec((512, D), lambda i: (i, 0)), ANYWHERE, whole(1, D)],
        ANYWHERE,
        shape(T, D),
        [
            pltpu.VMEM((T + SHORT + 8, D), f32), pltpu.VMEM((T, D), bf16),
            pltpu.VMEM((T, D), bf16),
            pltpu.SemaphoreType.DMA((1,)), pltpu.SemaphoreType.DMA((10,)),
        ],
        us=0.1,
    )(start, activ, w_down, middle, bias)


def bucket_edges(bucket_count, reach_max):
    exact_count = bucket_count // 2
    edge_list = list(range(1, exact_count + 1))
    distance = np.arange(exact_count, 64 * reach_max)
    level_of = exact_count + np.floor(
        np.log(distance / exact_count)
        / np.log(reach_max / exact_count)
        * (bucket_count - exact_count)
    ).astype(np.int64)
    for bucket_id in range(exact_count + 1, bucket_count):
        edge_list.append(int(distance[np.argmax(level_of >= bucket_id)]))
    return edge_list


EDGES = np.array(bucket_edges(NBUCKET, MAXDIST))
BUCKET = np.array([int(np.sum(n >= EDGES)) for n in range(256)])


def onehot_bucket(distance, live):
    hot = (np.arange(NBUCKET)[:, None] == BUCKET[distance][None, :]) & live[None, :]
    return hot.astype(np.float32)


def swap(a, bit):
    return lax.ppermute(a, "fsdp", [(i, i ^ bit) for i in range(8)])


def swap_rep(a, bit):
    return lax.ppermute(a, "rep", [(i, i ^ bit) for i in range(4)])


def gather_small(small):
    n = lax.axis_size("fsdp")
    if n != 8:
        return lax.all_gather(small, "fsdp", axis=0)
    me = lax.axis_index("fsdp")
    held = small[None]
    for bit in (1, 2, 4):
        other = swap(held, bit)
        upper = (me & bit) != 0
        held = jnp.concatenate(
            [jnp.where(upper, other, held), jnp.where(upper, held, other)], axis=0
        )
    return held


def after(value, *others):
    return lax.optimization_barrier((value,) + others)[0]


def after_all(values, *others):
    return lax.optimization_barrier(tuple(values) + others)[: len(values)]


def local(
    tokens, item_lengths, attn_gain, attn_shift, w_qkv, rel_table, w_out,
    ffn_gain, ffn_shift, w_up, up_bias, w_down, down_bias, cotangent,
):
    gather = lambda a: lax.all_gather(a, "fsdp", axis=0, tiled=True)
    pieces = (attn_gain, attn_shift, ffn_gain, ffn_shift, down_bias, up_bias, rel_table.reshape(-1))
    cuts = np.cumsum([0] + [piece.size for piece in pieces])
    rows = -(-int(cuts[-1]) // 2048) * 16
    small = jnp.concatenate(pieces + (jnp.zeros((rows * 128 - int(cuts[-1]),), bf16),))
    small_full = gather_small(small.reshape(rows, 128))
    ways = small_full.shape[0]
    small_full = small_full.reshape(ways, rows * 128)
    me = lax.axis_index("fsdp").astype(jnp.int32).reshape(1)
    by_pieces = ways == 8 and lax.axis_size("rep") == 4
    lens = item_lengths[0]
    first, second = lens[0], lens[1]
    long_first = first == LONG
    long_mid = second == LONG
    start = jnp.where(long_first, 0, jnp.where(long_mid, first, first + second)).reshape(1)
    bound = jnp.where(long_first, second, jnp.where(long_mid, lens[2], first)).reshape(1)
    tok, cot, grad_down_bias = prep(start, tokens, cotangent)
    out_up_own = jnp.concatenate([w_out, w_up], axis=1)
    if by_pieces:
        from_core, from_x, from_y = swap(w_qkv, 1), swap(w_qkv, 2), swap(w_qkv, 4)
        from_x, from_y = after_all((from_x, from_y), tok, out_up_own)
        top, bottom = swap(from_x[:64], 4), swap(from_y[64:], 2)
        out_up_own = after(out_up_own, top, bottom)
        qkv_pieces = (
            w_qkv, from_core, from_x, from_y, top, bottom,
            swap(from_x, 1), swap(from_y, 1), swap(top, 1), swap(bottom, 1),
        )
    out_up = gather(out_up_own)
    part = lambda i: small_full[:, cuts[i] : cuts[i + 1]].reshape(1, -1).astype(f32)
    gain_one, shift_one, gain_two, shift_two, down_bias_full, up_bias_full = (
        part(i) for i in range(6)
    )
    table = part(6).reshape(NBUCKET, H)
    relative = table - table[NBUCKET - 1 :]
    reach = np.arange(256)
    bias = jnp.dot(
        relative.T, onehot_bucket(reach, reach < 129),
        precision=lax.Precision.HIGHEST, preferred_element_type=f32,
    ).reshape(8, 2, 256)

    scatter = lambda a: lax.psum_scatter(a, "fsdp", scatter_dimension=0, tiled=True)
    total = lambda a: lax.psum(a, "rep")

    if by_pieces:
        qkv_pieces = after_all(qkv_pieces, bias, gain_two)
        packed, normed, qkv_full = qkv_forward_pieces(me, tok, gain_one, shift_one, qkv_pieces)
    else:
        qkv_full = gather(w_qkv)
        packed, normed = qkv_forward(tok, gain_one, shift_one, qkv_full)

    def second(mine, other):
        a_send, a_keep, b_send, b_keep = core_sum(mine, other)
        return a_keep, swap(a_send, 2), b_keep, swap(b_send, 4)

    def third(parts):
        a_send, a_keep, b_send, b_keep = pair_sum(*parts)
        return a_keep, swap(a_send, 4), b_keep, swap(b_send, 2)

    place = lax.axis_index("rep").astype(jnp.int32).reshape(1)

    mixed, query_aug = attn_fwd(packed, bias, bound)
    down_full = gather(after(w_down, mixed, out_up))
    middle, normed_two = out_forward(mixed, out_up, tok, gain_two, shift_two)
    activ, slope = up_forward(normed_two, out_up, up_bias_full)
    grad_w_ffn = grad_down(activ, cot, ways)
    grad_pre, grad_up_bias = grad_pre_of(after(cot, grad_w_ffn), down_full, slope)
    grad_w_ffn = grad_up(normed_two, grad_pre, grad_w_ffn, ways)
    share_ffn = scatter(grad_w_ffn)
    grad_att, grad_mixed, grad_ffn_gain, grad_ffn_shift = grad_middle_of(
        after(grad_pre, grad_w_ffn), out_up, middle, cot, gain_two
    )
    low, reach_low = attn_bwd(packed, query_aug, mixed, grad_mixed, bias, bound, 0)
    if by_pieces:
        low_theirs, low_mine = grad_blocks(me, (normed, mixed), (low, grad_att))
        low_other = swap(low_theirs, 1)
        packed_next = after(packed, low_mine)
    else:
        packed_next = after(packed, low)
    high, reach_high = attn_bwd(packed_next, query_aug, mixed, grad_mixed, bias, bound, 1)
    grad_reach = jnp.concatenate([reach_low, reach_high], axis=0)
    near_hot = onehot_bucket(reach, reach < EDGES[-1])
    grad_near = jnp.dot(
        near_hot, grad_reach.reshape(H, 256).T,
        precision=lax.Precision.HIGHEST, preferred_element_type=f32,
    )
    far = (np.arange(NBUCKET) == NBUCKET - 1).astype(np.float32)[:, None]
    grad_rel_table = grad_near - far * jnp.sum(grad_near, axis=0, keepdims=True)
    if by_pieces:
        high_theirs, high_mine = grad_blocks(me, (normed,), (high,))
        high_other = swap(high_theirs, 1)
        high_next = after(high, high_mine)
    else:
        share_low = scatter(grad_columns(normed, low))
        share_high = scatter(grad_columns(normed, high))
        share_out = scatter(grad_columns(mixed, grad_att))
        high_next = high
    grad_tokens, grad_attn_gain, grad_attn_shift = grad_tokens_of(
        start, low, high_next, qkv_full, tok, grad_att, gain_one
    )
    sum_down, sum_up = widen(total(after(share_ffn, grad_tokens)))
    flat = lambda a: a.reshape(ways, -1)
    vectors = jnp.concatenate(
        [
            flat(grad_attn_gain), flat(grad_attn_shift), flat(grad_ffn_gain),
            flat(grad_ffn_shift), flat(grad_down_bias), flat(grad_up_bias), flat(grad_rel_table),
        ],
        axis=1,
    )
    activ_next = after(activ, grad_tokens)
    if by_pieces:
        for bit in (1, 2, 4):
            vectors = vectors + swap(vectors, bit)
        mine = lax.dynamic_slice_in_dim(vectors, lax.axis_index("fsdp"), 1, 0).reshape(-1)
        mine = jnp.concatenate([mine, jnp.zeros((128 * 128 - mine.size,), f32)])
        low_parts = second(after(low_mine, grad_tokens), low_other)
        high_parts = second(after(high_mine, low_parts[0]), high_other)
        low_parts = third(after_all(low_parts, high_parts[0]))
        high_parts = third(after_all(high_parts, low_parts[0]))
        send, keep = last_sum(
            place, mine.astype(bf16).reshape(128, 128), *low_parts, *high_parts
        )
        got = swap_rep(send, 1)
        activ_next = after(activ_next, keep)
    output = output_of(start, activ_next, down_full, middle, down_bias_full)
    if by_pieces:
        send, keep = half_sum(place, *after_all((keep, got), output))
        own = quarter_sum(after(keep, sum_up), swap_rep(send, 2))
        near = swap_rep(own, 2)
        far = swap_rep(jnp.concatenate([own, near], axis=0), 1)
        sum_qkv, sum_out, mine = spread(place, own, near, far)
        mine = mine.reshape(1, -1)
    else:
        mine = total(scatter(vectors))
        sum_out = total(share_out).astype(f32)
        sum_qkv = jnp.stack(
            [total(share_low).reshape(-1, 3, 512), total(share_high).reshape(-1, 3, 512)], axis=2
        ).reshape(-1, 3 * D).astype(f32)
    cut = lambda i: mine[0, cuts[i] : cuts[i + 1]].astype(f32)
    return (
        output, grad_tokens, cut(0), cut(1), sum_qkv, cut(6).reshape(-1, H),
        sum_out, cut(2), cut(3), sum_up, cut(5), sum_down, cut(4),
    )


def solution(mesh):
    rows, vec, mat = P(("rep", "fsdp"), None), P("fsdp"), P("fsdp", None)
    in_specs = (rows, rows, vec, vec, mat, mat, mat, vec, vec, mat, vec, mat, vec, rows)
    out_specs = (rows, rows, vec, vec, mat, mat, mat, vec, vec, mat, vec, mat, vec)
    return jax.shard_map(local, mesh=mesh, in_specs=in_specs, out_specs=out_specs, check_vma=False)
```

```python
import functools

import jax
import jax.numpy as jnp
import numpy as np
from jax import lax
from jax.experimental import pallas as pl
from jax.experimental.pallas import tpu as pltpu
from jax.sharding import PartitionSpec as P

D = 1024
H = 16
HD = 64
FF = 4096
NBUCKET = 32
MAXDIST = 128
bf16 = jnp.bfloat16
f32 = jnp.float32
NEG = -1e9
LONG = 1024
SHORT = 256
T = 1280
NN = (((1,), (0,)), ((), ()))
NT = (((1,), (1,)), ((), ()))
TN = (((0,), (0,)), ((), ()))


def dot(a, b, dims):
    return lax.dot_general(a, b, dims, preferred_element_type=f32)


def split3(x):
    a = x.astype(bf16)
    r = x - a.astype(f32)
    b = r.astype(bf16)
    return a, b, (r - b.astype(f32)).astype(bf16)


def near_band(g):
    r = lax.broadcasted_iota(jnp.int32, (128, 256), 0)
    c = lax.broadcasted_iota(jnp.int32, (128, 256), 1)
    return jnp.where(c < r, NEG, pltpu.roll(jnp.broadcast_to(g, (128, 256)), 0, 1, stride=1, stride_axis=0))


def fwd_body(bnd_ref, g_ref, q_ref, k_ref, v_ref, o_ref, qa_ref):
    lane = lax.broadcasted_iota(jnp.int32, (1, 128), 1)
    bnd = bnd_ref[0]
    bands = [near_band(g_ref[0, h : h + 1, :]) for h in range(2)]
    for blk in range(5):
        R = 256 * blk
        lo = 0 if blk < 4 else 1024
        nk = R + 256 - lo
        qrow = q_ref[R : R + 256, :] * bf16(0.125)
        outs = []
        for h in range(2):
            mine = (lane < 64) if h == 0 else (lane >= 64)
            band = bands[h]

            def visible(x, key, query):
                if blk < 4:
                    return x
                rr = lax.broadcasted_iota(jnp.int32, x.shape, 0) + key
                cc = lax.broadcasted_iota(jnp.int32, x.shape, 1) + query
                return jnp.where((cc >= bnd) & (rr < bnd), NEG, x)

            st = dot(k_ref[lo : R + 256, :], jnp.where(mine, qrow, bf16(0)), NT)
            pieces = []
            if nk > 384:
                pieces.append(st[: nk - 384])
            if nk > 256:
                edge = st[nk - 384 : nk - 256]
                pieces.append(
                    jnp.concatenate([edge[:, :128] + band[:, 128:], edge[:, 128:]], axis=1)
                )
            pieces.append(visible(st[nk - 256 : nk - 128] + band, 0, 0))
            last = visible(st[nk - 128 :, 128:] + band[:, :128], 128, 128)
            top = None
            for piece in pieces:
                m = jnp.max(piece, axis=0, keepdims=True)
                top = m if top is None else jnp.maximum(top, m)
            right = jnp.maximum(top[:, 128:], jnp.max(last, axis=0, keepdims=True))
            top = jnp.concatenate([top[:, :128], right], axis=1)
            probs = [jnp.exp(piece - top).astype(bf16) for piece in pieces]
            probs.append(
                jnp.concatenate(
                    [jnp.zeros((128, 128), bf16), jnp.exp(last - right).astype(bf16)], axis=1
                )
            )
            va = jnp.where(mine, v_ref[lo : R + 256, :], bf16(1))
            o = dot(jnp.concatenate(probs, axis=0), va, TN)
            outs.append(o)
            lse = jnp.transpose(jnp.broadcast_to(top, (128, 256))) + jnp.log(
                jnp.where(mine, 1.0, o)
            )
            a, b, c = split3(lse)
            base = 64 if h == 0 else 0
            qa_ref[R : R + 256, 128 * h : 128 * h + 128] = jnp.where(
                mine, qrow,
                jnp.where(lane == base, a, jnp.where(lane == base + 1, b, jnp.where(lane == base + 2, c, bf16(0)))),
            )
        total = pltpu.roll(jnp.where(lane < 64, outs[1], outs[0]), 64, 1)
        o_ref[R : R + 256, :] = (jnp.where(lane < 64, outs[0], outs[1]) / total).astype(bf16)

def attn_fwd(packed,g,bnd):
    return pl.pallas_call(fwd_body,
        grid=(8,),
        in_specs=[pl.BlockSpec(memory_space=pltpu.SMEM),
                  pl.BlockSpec((1,2,256),lambda i:(i,0,0)),
                  pl.BlockSpec((T,128),lambda i:(0,i)),
                  pl.BlockSpec((T,128),lambda i:(0,8+i)),
                  pl.BlockSpec((T,128),lambda i:(0,16+i))],
        out_specs=[pl.BlockSpec((T,128),lambda i:(0,i)),pl.BlockSpec((T,256),lambda i:(0,i))],
        out_shape=[jax.ShapeDtypeStruct((T,1024),bf16),jax.ShapeDtypeStruct((T,2048),bf16)],
        cost_estimate=cost(27),
        compiler_params=pltpu.CompilerParams(vmem_limit_bytes=48<<20))(bnd,g,packed,packed,packed)

def bwd_body(bnd_ref,g_ref,qa_ref,k_ref,v_ref,o_ref,do_ref,grad_ref,gs_ref,dq_acc,band_acc):
    lane=lax.broadcasted_iota(jnp.int32,(1,128),1)
    bnd=bnd_ref[0]
    r1=lax.broadcasted_iota(jnp.int32,(128,256),0); c1=lax.broadcasted_iota(jnp.int32,(128,256),1)
    prod=do_ref[...].astype(f32)*o_ref[...].astype(f32)
    ph=prod.astype(bf16); plo=(prod-ph.astype(f32)).astype(bf16)
    i0=lax.broadcasted_iota(jnp.int32,(128,128),0); j0=lax.broadcasted_iota(jnp.int32,(128,128),1)
    sw=jnp.where((i0<64)!=(j0<64),bf16(1),bf16(0))
    delta=-(dot(ph,sw,NN)+dot(plo,sw,NN))
    dh,dl,_=split3(delta)
    gks=[];gvs=[]
    for h in range(2):
        mine=(lane<64) if h==0 else (lane>=64)
        base=64 if h==0 else 0
        g=g_ref[0,h:h+1,:]
        band=pltpu.roll(jnp.broadcast_to(g,(128,256)),0,1,stride=1,stride_axis=0)
        band=jnp.where(c1<r1,NEG,band)
        dob=do_ref[...]
        doa=jnp.where(mine,dob,jnp.where(lane==base,dh,jnp.where(lane==base+1,dl,bf16(0))))
        gk=[];gv=[]
        for blk in (3,2,1,0,4):
            R=256*blk
            hi=1024 if blk<4 else 1280
            nq=hi-R
            neg=jnp.where((lane>=base)&(lane<base+3),bf16(-1),bf16(0))
            one=jnp.where((lane>=base)&(lane<base+2),bf16(1),bf16(0))
            ka=jnp.where(mine,k_ref[R:R+256,:],neg)
            va=jnp.where(mine,v_ref[R:R+256,:],one)
            qa=qa_ref[R:hi,128*h:128*h+128]
            do=doa[R:hi]
            st=dot(ka,qa,NT)
            dpt=dot(va,do,NT)
            pr=[];dr=[]
            for sub in range(2):
                b0=128*sub
                w=min(256,nq-b0)
                sb=st[b0:b0+128,b0:b0+w]+band[:,:w]
                if blk==4:
                    rr=lax.broadcasted_iota(jnp.int32,sb.shape,0)+b0
                    cc=lax.broadcasted_iota(jnp.int32,sb.shape,1)+b0
                    sb=jnp.where((cc>=bnd)&(rr<bnd),NEG,sb)
                pb=jnp.exp(sb)
                db=pb*dpt[b0:b0+128,b0:b0+w]
                if h==0 or True:
                    if blk==3 and sub==0: band_acc[...]=db
                    elif w==256: band_acc[...]+=db
                    else: band_acc[:,:w]+=db
                ps=[pb.astype(bf16)]; ds=[db.astype(bf16)]
                if sub==1:
                    ps.insert(0,jnp.zeros((128,128),bf16)); ds.insert(0,jnp.zeros((128,128),bf16))
                if b0+w<nq:
                    pf=jnp.exp(st[b0:b0+128,b0+w:])
                    df=pf*dpt[b0:b0+128,b0+w:]
                    ps.append(pf.astype(bf16)); ds.append(df.astype(bf16))
                pr.append(jnp.concatenate(ps,axis=1) if len(ps)>1 else ps[0])
                dr.append(jnp.concatenate(ds,axis=1) if len(ds)>1 else ds[0])
            p=jnp.concatenate(pr,axis=0); ds=jnp.concatenate(dr,axis=0)
            gvb=dot(p,do,NN); gkb=dot(ds,qa,NN)
            dqb=dot(ds,ka,TN)
            if blk in (3,2,1,0):
                dq_acc[h,R:R+256,:]=dqb[:256]
                if nq>256: dq_acc[h,R+256:hi,:]+=dqb[256:]
            else:
                dq_acc[h,R:hi,:]=dqb
            gk.append((R,gkb)); gv.append((R,gvb))
        gks.append(gk);gvs.append(gv)
        Y=band_acc[...]
        n=64
        while n>=1:
            Y=Y[:n]+pltpu.roll(Y[n:2*n],256-n,1)
            n//=2
        gs_ref[0,h:h+1,:]=Y
    for (R,a),(_,b) in zip(*gks): grad_ref[1,R:R+256,:]=jnp.where(lane<64,a,b).astype(bf16)
    for (R,a),(_,b) in zip(*gvs): grad_ref[2,R:R+256,:]=jnp.where(lane<64,a,b).astype(bf16)
    grad_ref[0]=(jnp.where(lane<64,dq_acc[0],dq_acc[1])*0.125).astype(bf16)

def attn_bwd(packed,qa,o,do,g,bnd,half):
    sp=lambda off: pl.BlockSpec((T,128),lambda i:(0,off+4*half+i))
    return pl.pallas_call(bwd_body,
        grid=(4,),
        in_specs=[pl.BlockSpec(memory_space=pltpu.SMEM),
                  pl.BlockSpec((1,2,256),lambda i:(4*half+i,0,0)),
                  pl.BlockSpec((T,256),lambda i:(0,4*half+i)),sp(8),sp(16),sp(0),sp(0)],
        out_specs=[pl.BlockSpec((3,T,128),lambda i:(0,0,i)),pl.BlockSpec((1,2,256),lambda i:(i,0,0))],
        out_shape=[jax.ShapeDtypeStruct((3,T,512),bf16),jax.ShapeDtypeStruct((4,2,256),f32)],
        scratch_shapes=[pltpu.VMEM((2,T,128),f32),pltpu.VMEM((128,256),f32)],
        cost_estimate=cost(22.5),
        compiler_params=pltpu.CompilerParams(vmem_limit_bytes=56<<20))(bnd,g,qa,packed,packed,o,do)


def shape(*dims, dtype=bf16):
    return jax.ShapeDtypeStruct(dims, dtype)


def whole(*dims):
    return pl.BlockSpec(dims, lambda i: (0,) * len(dims))


def columns(rows, width, first=0):
    return pl.BlockSpec((rows, width), lambda i: (0, first + i))


SCALAR = pl.BlockSpec(memory_space=pltpu.SMEM)


def cost(us):
    return pl.CostEstimate(flops=int(us * 1.15e9), bytes_accessed=0, transcendentals=0)


def call(body, grid, in_specs, out_specs, out_shape, scratch=(), us=1.0, aliases={}):
    return pl.pallas_call(
        body,
        grid=(grid,),
        in_specs=in_specs,
        out_specs=out_specs,
        out_shape=out_shape,
        scratch_shapes=list(scratch),
        input_output_aliases=aliases,
        cost_estimate=cost(us),
        compiler_params=pltpu.CompilerParams(vmem_limit_bytes=58 << 20),
    )


def row_stats(x):
    mean = jnp.mean(x, axis=-1, keepdims=True)
    center = x - mean
    rstd = lax.rsqrt(jnp.mean(center * center, axis=-1, keepdims=True) + 1e-05)
    return center * rstd, rstd


def back_through_norm(xhat, rstd, scaled):
    return rstd * (
        scaled
        - jnp.mean(scaled, axis=-1, keepdims=True)
        - xhat * jnp.mean(scaled * xhat, axis=-1, keepdims=True)
    )


def shifted_rows(ext, offset, r):
    fine = lax.rem(offset, 8)
    rows = ext[pl.ds(pl.multiple_of(offset - fine + r, 8), 136), :].reshape(17, 8, D)
    rows = pltpu.roll(rows, lax.rem(8 - fine, 8), 1)
    keep = lax.broadcasted_iota(jnp.int32, (1, 8, D), 1) < 8 - fine
    return jnp.where(keep, rows[:16], rows[1:]).reshape(128, D)


def prep_body(start_ref, tok_ref, cot_ref, tok_out, cot_out, bias_out, ext):
    start = start_ref[0]
    for source, target in ((tok_ref, tok_out), (cot_ref, cot_out)):
        for r in range(0, T, 256):
            ext[r : r + 256, :] = source[r : r + 256, :].astype(f32)
        ext[T : T + SHORT, :] = source[0:SHORT, :].astype(f32)
        total = None
        for r in range(0, T, 128):
            rows = shifted_rows(ext, start, r)
            target[r : r + 128, :] = rows.astype(bf16)
            if target is cot_out:
                part = jnp.sum(rows, axis=0, keepdims=True)
                total = part if total is None else total + part
    bias_out[...] = total


def prep(start, tokens, cotangent):
    return call(
        prep_body, 1,
        [SCALAR, whole(T, D), whole(T, D)],
        [whole(T, D), whole(T, D), whole(1, D)],
        [shape(T, D), shape(T, D), shape(1, D, dtype=f32)],
        [pltpu.VMEM((T + SHORT + 8, D), f32)],
        us=7,
    )(start, tokens, cotangent)


def qkv_body(tok_ref, gain_ref, shift_ref, w_ref, packed_ref, normed_ref):
    @pl.when(pl.program_id(0) == 0)
    def _():
        for r in range(0, T, 256):
            xhat, _ = row_stats(tok_ref[r : r + 256, :].astype(f32))
            normed_ref[r : r + 256, :] = (xhat * gain_ref[...] + shift_ref[...]).astype(bf16)

    packed_ref[...] = dot(normed_ref[...], w_ref[...], NN).astype(bf16)


def qkv_forward(tok, gain, shift, w_qkv):
    return call(
        qkv_body, 6,
        [whole(T, D), whole(1, D), whole(1, D), columns(D, 512)],
        [columns(T, 512), whole(T, D)],
        [shape(T, 3 * D), shape(T, D)],
        us=15,
    )(tok, gain, shift, w_qkv)


PIECES = (
    (0, 0, 128), (1, 0, 128), (2, 0, 128), (4, 0, 128), (6, 0, 64), (6, 64, 64),
    (3, 0, 128), (5, 0, 128), (7, 0, 64), (7, 64, 64),
)


def qkv_pieces_body(me_ref, tok_ref, gain_ref, shift_ref, *refs):
    pieces = refs[: len(PIECES)]
    packed_ref, normed_ref, w_out, w_all, arrived, left = refs[len(PIECES) :]
    step = pl.program_id(0)
    save = pltpu.make_async_copy(w_all, w_out, left)

    @pl.when(step == 0)
    def _():
        copies = []
        for n, (other, first, rows) in enumerate(PIECES):
            at = pl.multiple_of((me_ref[0] ^ other) * 128 + first, 64)
            copy = pltpu.make_async_copy(pieces[n], w_all.at[pl.ds(at, rows), :], arrived.at[n])
            copy.start()
            copies.append(copy)
        for r in range(0, T, 256):
            xhat, _ = row_stats(tok_ref[r : r + 256, :].astype(f32))
            normed_ref[r : r + 256, :] = (xhat * gain_ref[...] + shift_ref[...]).astype(bf16)
        for copy in copies:
            copy.wait()
        save.start()

    at = pl.multiple_of(step * 512, 512)
    packed_ref[...] = dot(normed_ref[...], w_all[:, pl.ds(at, 512)], NN).astype(bf16)

    @pl.when(step == pl.num_programs(0) - 1)
    def _():
        save.wait()


def qkv_forward_pieces(me, tok, gain, shift, pieces):
    anywhere = pl.BlockSpec(memory_space=pl.ANY)
    return call(
        qkv_pieces_body, 6,
        [SCALAR, whole(T, D), whole(1, D), whole(1, D)] + [anywhere] * len(PIECES),
        [columns(T, 512), whole(T, D), anywhere],
        [shape(T, 3 * D), shape(T, D), shape(D, 3 * D)],
        [
            pltpu.VMEM((D, 3 * D), bf16),
            pltpu.SemaphoreType.DMA((len(PIECES),)),
            pltpu.SemaphoreType.DMA,
        ],
        us=16,
    )(me, tok, gain, shift, *pieces)


def out_body(mixed_ref, w_ref, tok_ref, gain_ref, shift_ref, middle_ref, normed_ref):
    middle = tok_ref[...].astype(f32) + dot(mixed_ref[...], w_ref[...], NN)
    middle_ref[...] = middle.astype(bf16)
    xhat, _ = row_stats(middle)
    normed_ref[...] = (xhat * gain_ref[...] + shift_ref[...]).astype(bf16)


def out_forward(mixed, w_out_up, tok, gain, shift):
    rows = pl.BlockSpec((256, D), lambda i: (i, 0))
    return call(
        out_body, T // 256,
        [rows, whole(D, D), rows, whole(1, D), whole(1, D)],
        [rows, rows],
        [shape(T, D), shape(T, D)],
        us=8.6,
    )(mixed, w_out_up, tok, gain, shift)


C0 = float(np.sqrt(2.0 / np.pi))
C1 = 0.044715 * C0


def up_body(normed_ref, w_ref, bias_ref, activ_ref, slope_ref, *held):
    chunks = [(r, c) for c in range(0, 512, 256) for r in range(0, T, 128)]

    def finish(n, later):
        r, c = chunks[n]
        bias = bias_ref[:, c : c + 256]
        if later is not None:
            bias = bias + 0.0 * held[later % 6][120:121, :]
        for q in range(0, 128, 16):
            u = held[n % 6][q : q + 16, :] + bias
            square = u * u
            half = 0.5 * jnp.tanh(u * (C0 + C1 * square)) + 0.5
            activ = u * half
            activ_ref[r + q : r + q + 16, c : c + 256] = activ.astype(bf16)
            slope = half + activ * (1.0 - half) * (2.0 * C0 + 6.0 * C1 * square)
            slope_ref[r + q : r + q + 16, c : c + 256] = slope.astype(bf16)

    for n, (r, c) in enumerate(chunks):
        held[n % 6][...] = dot(normed_ref[r : r + 128, :], w_ref[:, c : c + 256], NN)
        if n >= 2:
            finish(n - 2, n - 1)
    finish(len(chunks) - 2, None)
    finish(len(chunks) - 1, None)


def up_forward(normed_two, w_out_up, up_bias):
    return call(
        up_body, 8,
        [whole(T, D), columns(D, 512, 2), columns(1, 512)],
        [columns(T, 512), columns(T, 512)],
        [shape(T, FF), shape(T, FF)],
        [pltpu.VMEM((128, 256), f32)] * 6,
        us=21.3,
    )(normed_two, w_out_up, up_bias)


def grad_down_body(activ_ref, cot_ref, out_ref):
    out_ref[0, 0] = dot(activ_ref[...], cot_ref[...], TN).astype(bf16).reshape(out_ref.shape[2:])


def ffn_shape(ways):
    return shape(ways, 2, 4, D // ways, D)


def grad_down(activ, cot, ways):
    rows = FF // ways
    return call(
        grad_down_body, ways,
        [columns(T, rows), whole(T, D)],
        pl.BlockSpec((1, 1, 4, D // ways, D), lambda i: (i, 0, 0, 0, 0)),
        ffn_shape(ways),
        us=16.3,
    )(activ, cot)


def grad_up_body(left_ref, right_ref, held_ref, out_ref):
    value = dot(left_ref[...], right_ref[...], TN).astype(bf16)
    out_ref[...] = value.reshape(out_ref.shape)


def grad_up(left, right, held, ways):
    return call(
        grad_up_body, 8,
        [whole(T, D), columns(T, 512), pl.BlockSpec(memory_space=pl.ANY)],
        pl.BlockSpec((ways, 1, 1, D // ways, 512), lambda i: (0, 1, i // 2, 0, i % 2)),
        ffn_shape(ways),
        us=16.3, aliases={2: 0},
    )(left, right, held)


def grad_pre_body(cot_ref, w_ref, slope_ref, pre_ref, bias_ref):
    total = None
    for r in range(0, T, 256):
        pre = (
            dot(cot_ref[r : r + 256, :], w_ref[...], NT) * slope_ref[r : r + 256, :].astype(f32)
        ).astype(bf16)
        pre_ref[r : r + 256, :] = pre
        part = jnp.sum(pre.astype(f32), axis=0, keepdims=True)
        total = part if total is None else total + part
    bias_ref[...] = total


def grad_pre_of(cot, w_down, slope):
    return call(
        grad_pre_body, 8,
        [whole(T, D), pl.BlockSpec((512, D), lambda i: (i, 0)), columns(T, 512)],
        [columns(T, 512), columns(1, 512)],
        [shape(T, FF), shape(1, FF, dtype=f32)],
        us=19,
    )(cot, w_down, slope)


def grad_tile_body(left_ref, right_ref, out_ref):
    right = right_ref[...]
    right = right.reshape(right.shape[-2:])
    out_ref[...] = dot(left_ref[...], right, TN).astype(bf16)


def right_tiles(right):
    if right.ndim == 3:
        return right.shape[0], pl.BlockSpec((1, T, 512), lambda i: (i, 0, 0))
    return right.shape[1] // 512, columns(T, 512)


def grad_columns(left, right):
    tiles, spec = right_tiles(right)
    return call(
        grad_tile_body, tiles,
        [whole(T, D), spec],
        columns(D, 512),
        shape(D, tiles * 512),
        us=2.0 * tiles,
    )(left, right)


def take_blocks(me, left_ref, held):
    for n in range(8):
        core = (me & 1) if n >= 4 else 1 - (me & 1)
        at = pl.multiple_of((((me >> 1) ^ (n % 4)) * 2 + core) * 128, 128)
        held[:, 128 * n : 128 * n + 128] = left_ref[:, pl.ds(at, 128)]


def grad_blocks(me, lefts, rights):
    specs, begins, first = [SCALAR], [], 0
    for right in rights:
        if right.ndim == 3:
            count = right.shape[0]
            spec = pl.BlockSpec(
                (1, T, 512), lambda i, a=first, n=count: (jnp.clip(i - a, 0, n - 1), 0, 0)
            )
        else:
            count = right.shape[1] // 512
            spec = pl.BlockSpec(
                (T, 512), lambda i, a=first, n=count: (0, jnp.clip(i - a, 0, n - 1))
            )
        specs.append(spec)
        begins.append(first)
        first += count
    n, tiles = len(lefts), first

    def body(me_ref, *refs):
        theirs, mine, held = refs[2 * n :]
        step = pl.program_id(0)
        for begin, end, left_ref, right_ref in zip(
            begins, begins[1:] + [tiles], refs[n : 2 * n], refs[:n]
        ):

            @pl.when(step == begin)
            def _():
                take_blocks(me_ref[0], left_ref, held)

            @pl.when((step >= begin) & (step < end))
            def _():
                right = right_ref[...]
                value = dot(held[...], right.reshape(right.shape[-2:]), TN).astype(bf16)
                theirs[...] = value[:512]
                mine[...] = value[512:]

    return call(
        body, tiles, specs + [whole(T, D)] * n, [columns(512, 512)] * 2,
        [shape(512, tiles * 512)] * 2,
        [pltpu.VMEM((T, D), bf16)],
        us=1.5 + 2.3 * tiles,
    )(me, *rights, *lefts)


def core_sum_body(mine, other, a_send, a_keep, b_send, b_keep):
    for rel, a, b, place_a, place_b in (
        (0, a_keep, b_keep, 0, 0), (1, a_send, b_keep, 0, 1),
        (2, a_keep, b_send, 1, 0), (3, a_send, b_send, 1, 1),
    ):
        rows = slice(128 * rel, 128 * rel + 128)
        total = (mine[rows, :].astype(f32) + other[rows, :].astype(f32)).astype(bf16)
        a[place_a] = total[:, :256]
        b[place_b] = total[:, 256:]


def core_sum(mine, other):
    tiles = mine.shape[1] // 512
    part = pl.BlockSpec((2, 128, 256), lambda i: (0, 0, i))
    return call(
        core_sum_body, tiles, [columns(512, 512)] * 2, [part] * 4,
        [shape(2, 128, tiles * 256)] * 4,
        us=0.1,
    )(mine, other)


def pair_sum_body(a_keep, a_got, b_keep, b_got, a_send, a_rest, b_send, b_rest):
    for keep, got, send, rest in ((a_keep, a_got, a_send, a_rest), (b_keep, b_got, b_send, b_rest)):
        for place, target in ((1, send), (0, rest)):
            target[...] = (keep[place].astype(f32) + got[place].astype(f32)).astype(bf16)


def pair_sum(*parts):
    width = parts[0].shape[2]
    return call(
        pair_sum_body, 1,
        [whole(2, 128, width)] * 4,
        [whole(128, width)] * 4,
        [shape(128, width)] * 4,
        us=0.1,
    )(*parts)


def add(a_ref, b_ref):
    return a_ref[...].astype(f32) + b_ref[...].astype(f32)


def last_sum_body(place_ref, small, *refs):
    *parts, send, keep = refs
    bit = place_ref[0] & 1
    first = 0
    for n in range(0, len(parts), 4):
        for lane, (one, two) in enumerate((parts[n : n + 2], parts[n + 2 : n + 4])):
            for target, mine in ((keep, bit), (send, 1 - bit)):
                at = pl.ds(pl.multiple_of(mine * 64, 64), 64)
                total = (one[at, :].astype(f32) + two[at, :].astype(f32)).astype(bf16)
                for tile in range(total.shape[1] // 256):
                    to = first + 512 * tile + 256 * lane
                    target[:, to : to + 256] = total[:, 256 * tile : 256 * tile + 256]
        first += 2 * parts[n].shape[1]
    for target, mine in ((keep, bit), (send, 1 - bit)):
        target[:, first:] = small[pl.ds(pl.multiple_of(mine * 64, 64), 64), :]


def last_sum(place, small, *parts):
    width = sum(part.shape[1] for part in parts) // 2 + small.shape[1]
    return call(
        last_sum_body, 1,
        [SCALAR] + [whole(*part.shape) for part in (small,) + parts],
        [whole(64, width)] * 2,
        [shape(64, width)] * 2,
        us=0.1,
    )(place, small, *parts)


def half_sum_body(place_ref, keep, got, send, rest):
    bit = place_ref[0] >> 1
    rows = send.shape[0]
    for target, mine in ((rest, bit), (send, 1 - bit)):
        at = pl.ds(pl.multiple_of(mine * rows, rows), rows)
        target[...] = (keep[at, :].astype(f32) + got[at, :].astype(f32)).astype(bf16)


def half_sum(place, keep, got):
    rows, width = keep.shape
    return call(
        half_sum_body, 1,
        [SCALAR] + [whole(rows, width)] * 2,
        [whole(rows // 2, width)] * 2,
        [shape(rows // 2, width)] * 2,
        us=0.1,
    )(place, keep, got)


def quarter_sum_body(keep, got, out):
    out[...] = (keep[...].astype(f32) + got[...].astype(f32)).astype(bf16)


def quarter_sum(keep, got):
    return call(
        quarter_sum_body, 1, [whole(*keep.shape)] * 2, whole(*keep.shape), shape(*keep.shape),
        us=0.1,
    )(keep, got)


def quarters(place_ref, own, near, far):
    one, two, rows = place_ref[0] & 1, place_ref[0] >> 1, own.shape[0]
    for ref, cut, bit_one, bit_two in (
        (own, slice(0, rows), one, two),
        (near, slice(0, rows), one, 1 - two),
        (far, slice(0, rows), 1 - one, two),
        (far, slice(rows, 2 * rows), 1 - one, 1 - two),
    ):
        yield ref, cut, pl.ds(pl.multiple_of((bit_one * 2 + bit_two) * rows, rows), rows)


def spread_body(place_ref, own, near, far, qkv_out, out_out, small_out):
    for ref, cut, at in quarters(place_ref, own, near, far):
        for half, start in ((0, 0), (1, 2560)):
            for n in range(3):
                to = 1024 * n + 512 * half
                qkv_out[at, to : to + 512] = ref[
                    cut, start + 512 * n : start + 512 * n + 512
                ].astype(f32)
        out_out[at, :] = ref[cut, 1536:2560].astype(f32)
        small_out[at, :] = ref[cut, 4 * D :].astype(f32)


def spread(place, *parts):
    return call(
        spread_body, 1,
        [SCALAR] + [whole(*part.shape) for part in parts],
        [whole(128, 3 * D), whole(128, D), whole(128, 128)],
        [shape(128, 3 * D, dtype=f32), shape(128, D, dtype=f32), shape(128, 128, dtype=f32)],
        us=0.1,
    )(place, *parts)


def widen_body(sum_ref, down_ref, up_ref):
    rows = sum_ref.shape[3]
    for k in range(4):
        down_ref[rows * k : rows * k + rows, :] = sum_ref[0, 0, k].astype(f32)
        up_ref[:, D * k : D * k + D] = sum_ref[0, 1, k].astype(f32)


def widen(total):
    rows = total.shape[3]
    return call(
        widen_body, 1,
        [whole(*total.shape)],
        [whole(4 * rows, D), whole(rows, FF)],
        [shape(4 * rows, D, dtype=f32), shape(rows, FF, dtype=f32)],
        us=0.1,
    )(total)


ANYWHERE = pl.BlockSpec(memory_space=pl.ANY)


def fetch(pairs, sems):
    return [pltpu.make_async_copy(one, two, sems.at[n]) for n, (one, two) in enumerate(pairs)]


def mid_body(
    pre_ref, up_ref, middle_any, cot_any, gain_ref, out_up_any,
    att_any, mixed_any, gain_out, shift_out, acc, middle, cot, w_out, att, mixed, got, put,
):
    step = pl.program_id(0)
    loads = fetch(
        ((middle_any, middle), (cot_any, cot), (out_up_any.at[:, pl.ds(0, D)], w_out)), got
    )

    @pl.when(step == 0)
    def _():
        for load in loads:
            load.start()
        acc[...] = dot(pre_ref[...], up_ref[...], NT)

    @pl.when(step > 0)
    def _():
        acc[...] += dot(pre_ref[...], up_ref[...], NT)

    @pl.when(step == pl.num_programs(0) - 1)
    def _():
        for load in loads:
            load.wait()
        gains = shifts = None
        stores = []
        for n, r in enumerate(range(0, T, 256)):
            rows = slice(r, r + 256)
            g = acc[rows, :]
            xhat, rstd = row_stats(middle[rows, :].astype(f32))
            a = jnp.sum(g * xhat, axis=0, keepdims=True)
            b = jnp.sum(g, axis=0, keepdims=True)
            gains = a if gains is None else gains + a
            shifts = b if shifts is None else shifts + b
            mid = cot[rows, :].astype(f32) + back_through_norm(xhat, rstd, g * gain_ref[...])
            att[rows, :] = mid.astype(bf16)
            mixed[rows, :] = dot(att[rows, :], w_out[...], NT).astype(bf16)
            for one, two, sem in ((att, att_any, 2 * n), (mixed, mixed_any, 2 * n + 1)):
                store = pltpu.make_async_copy(
                    one.at[pl.ds(r, 256), :], two.at[pl.ds(r, 256), :], put.at[sem]
                )
                store.start()
                stores.append(store)
        gain_out[...] = gains
        shift_out[...] = shifts
        for store in stores:
            store.wait()


def grad_middle_of(grad_pre, w_out_up, middle, cot, gain):
    return call(
        mid_body, 8,
        [columns(T, 512), columns(D, 512, 2), ANYWHERE, ANYWHERE, whole(1, D), ANYWHERE],
        [ANYWHERE, ANYWHERE, whole(1, D), whole(1, D)],
        [shape(T, D), shape(T, D), shape(1, D, dtype=f32), shape(1, D, dtype=f32)],
        [
            pltpu.VMEM((T, D), f32), pltpu.VMEM((T, D), bf16), pltpu.VMEM((T, D), bf16),
            pltpu.VMEM((D, D), bf16), pltpu.VMEM((T, D), bf16), pltpu.VMEM((T, D), bf16),
            pltpu.SemaphoreType.DMA((3,)), pltpu.SemaphoreType.DMA((10,)),
        ],
        us=23.5,
    )(grad_pre, w_out_up, middle, cot, gain, w_out_up)


def unrotate(ext, start, staged, out_any, sems):
    ext[0:SHORT, :] = ext[T : T + SHORT, :]
    stores = []
    for n, r in enumerate(range(0, T, 128)):
        staged[r : r + 128, :] = shifted_rows(ext, SHORT - start, r).astype(bf16)
        store = pltpu.make_async_copy(
            staged.at[pl.ds(r, 128), :], out_any.at[pl.ds(r, 128), :], sems.at[n]
        )
        store.start()
        stores.append(store)
    for store in stores:
        store.wait()


def tok_body(
    start_ref, low_ref, high_ref, w_ref, tok_any, mid_any, gain_ref,
    grad_any, gain_out, shift_out, ext, tok, mid, staged, got, put,
):
    step = pl.program_id(0)
    loads = fetch(((tok_any, tok), (mid_any, mid)), got)

    @pl.when(step == 0)
    def _():
        for load in loads:
            load.start()
        ext[SHORT : SHORT + T, :] = dot(low_ref[0], w_ref[...], NT)

    @pl.when((step > 0) & (lax.rem(step, 2) == 0))
    def _():
        ext[SHORT : SHORT + T, :] += dot(low_ref[0], w_ref[...], NT)

    @pl.when(lax.rem(step, 2) == 1)
    def _():
        ext[SHORT : SHORT + T, :] += dot(high_ref[0], w_ref[...], NT)

    @pl.when(step == pl.num_programs(0) - 1)
    def _():
        for load in loads:
            load.wait()
        gains = shifts = None
        for r in range(0, T, 256):
            g = ext[SHORT + r : SHORT + r + 256, :]
            xhat, rstd = row_stats(tok[r : r + 256, :].astype(f32))
            a = jnp.sum(g * xhat, axis=0, keepdims=True)
            b = jnp.sum(g, axis=0, keepdims=True)
            gains = a if gains is None else gains + a
            shifts = b if shifts is None else shifts + b
            ext[SHORT + r : SHORT + r + 256, :] = mid[r : r + 256, :].astype(f32) + (
                back_through_norm(xhat, rstd, g * gain_ref[...])
            )
        gain_out[...] = gains
        shift_out[...] = shifts
        unrotate(ext, start_ref[0], staged, grad_any, put)


def grad_tokens_of(start, low, high, w_qkv, tok, mid, gain):
    half = pl.BlockSpec((1, T, 512), lambda i: (i // 2, 0, 0))
    return call(
        tok_body, 6,
        [SCALAR, half, half, columns(D, 512), ANYWHERE, ANYWHERE, whole(1, D)],
        [ANYWHERE, whole(1, D), whole(1, D)],
        [shape(T, D), shape(1, D, dtype=f32), shape(1, D, dtype=f32)],
        [
            pltpu.VMEM((T + SHORT + 8, D), f32), pltpu.VMEM((T, D), bf16),
            pltpu.VMEM((T, D), bf16), pltpu.VMEM((T, D), bf16),
            pltpu.SemaphoreType.DMA((2,)), pltpu.SemaphoreType.DMA((10,)),
        ],
        us=0.1,
    )(start, low, high, w_qkv, tok, mid, gain)


def output_body(
    start_ref, activ_ref, w_ref, middle_any, bias_ref, out_any, ext, middle, staged, got, put
):
    step = pl.program_id(0)
    loads = fetch(((middle_any, middle),), got)

    @pl.when(step == 0)
    def _():
        loads[0].start()
        ext[SHORT : SHORT + T, :] = dot(activ_ref[...], w_ref[...], NN)

    @pl.when(step > 0)
    def _():
        ext[SHORT : SHORT + T, :] += dot(activ_ref[...], w_ref[...], NN)

    @pl.when(step == pl.num_programs(0) - 1)
    def _():
        loads[0].wait()
        for r in range(0, T, 256):
            ext[SHORT + r : SHORT + r + 256, :] += (
                middle[r : r + 256, :].astype(f32) + bias_ref[...]
            )
        unrotate(ext, start_ref[0], staged, out_any, put)


def output_of(start, activ, w_down, middle, bias):
    return call(
        output_body, 8,
        [SCALAR, columns(T, 512), pl.BlockSpec((512, D), lambda i: (i, 0)), ANYWHERE, whole(1, D)],
        ANYWHERE,
        shape(T, D),
        [
            pltpu.VMEM((T + SHORT + 8, D), f32), pltpu.VMEM((T, D), bf16),
            pltpu.VMEM((T, D), bf16),
            pltpu.SemaphoreType.DMA((1,)), pltpu.SemaphoreType.DMA((10,)),
        ],
        us=0.1,
    )(start, activ, w_down, middle, bias)


def bucket_edges(bucket_count, reach_max):
    exact_count = bucket_count // 2
    edge_list = list(range(1, exact_count + 1))
    distance = np.arange(exact_count, 64 * reach_max)
    level_of = exact_count + np.floor(
        np.log(distance / exact_count)
        / np.log(reach_max / exact_count)
        * (bucket_count - exact_count)
    ).astype(np.int64)
    for bucket_id in range(exact_count + 1, bucket_count):
        edge_list.append(int(distance[np.argmax(level_of >= bucket_id)]))
    return edge_list


EDGES = np.array(bucket_edges(NBUCKET, MAXDIST))
BUCKET = np.array([int(np.sum(n >= EDGES)) for n in range(256)])


def onehot_bucket(distance, live):
    hot = (np.arange(NBUCKET)[:, None] == BUCKET[distance][None, :]) & live[None, :]
    return hot.astype(np.float32)


def swap(a, bit):
    return lax.ppermute(a, "fsdp", [(i, i ^ bit) for i in range(8)])


def swap_rep(a, bit):
    return lax.ppermute(a, "rep", [(i, i ^ bit) for i in range(4)])


def gather_small(small):
    n = lax.axis_size("fsdp")
    if n != 8:
        return lax.all_gather(small, "fsdp", axis=0)
    me = lax.axis_index("fsdp")
    held = small[None]
    for bit in (1, 2, 4):
        other = swap(held, bit)
        upper = (me & bit) != 0
        held = jnp.concatenate(
            [jnp.where(upper, other, held), jnp.where(upper, held, other)], axis=0
        )
    return held


def after(value, *others):
    return lax.optimization_barrier((value,) + others)[0]


def after_all(values, *others):
    return lax.optimization_barrier(tuple(values) + others)[: len(values)]


def local(
    tokens, item_lengths, attn_gain, attn_shift, w_qkv, rel_table, w_out,
    ffn_gain, ffn_shift, w_up, up_bias, w_down, down_bias, cotangent,
):
    gather = lambda a: lax.all_gather(a, "fsdp", axis=0, tiled=True)
    pieces = (attn_gain, attn_shift, ffn_gain, ffn_shift, down_bias, up_bias, rel_table.reshape(-1))
    cuts = np.cumsum([0] + [piece.size for piece in pieces])
    rows = -(-int(cuts[-1]) // 2048) * 16
    small = jnp.concatenate(pieces + (jnp.zeros((rows * 128 - int(cuts[-1]),), bf16),))
    small_full = gather_small(small.reshape(rows, 128))
    ways = small_full.shape[0]
    small_full = small_full.reshape(ways, rows * 128)
    me = lax.axis_index("fsdp").astype(jnp.int32).reshape(1)
    by_pieces = ways == 8 and lax.axis_size("rep") == 4
    lens = item_lengths[0]
    first, second = lens[0], lens[1]
    long_first = first == LONG
    long_mid = second == LONG
    start = jnp.where(long_first, 0, jnp.where(long_mid, first, first + second)).reshape(1)
    bound = jnp.where(long_first, second, jnp.where(long_mid, lens[2], first)).reshape(1)
    tok, cot, grad_down_bias = prep(start, tokens, cotangent)
    out_up_own = jnp.concatenate([w_out, w_up], axis=1)
    if by_pieces:
        from_core, from_x, from_y = swap(w_qkv, 1), swap(w_qkv, 2), swap(w_qkv, 4)
        from_x, from_y = after_all((from_x, from_y), tok, out_up_own)
        top, bottom = swap(from_x[:64], 4), swap(from_y[64:], 2)
        out_up_own = after(out_up_own, top, bottom)
        qkv_pieces = (
            w_qkv, from_core, from_x, from_y, top, bottom,
            swap(from_x, 1), swap(from_y, 1), swap(top, 1), swap(bottom, 1),
        )
    out_up = gather(out_up_own)
    part = lambda i: small_full[:, cuts[i] : cuts[i + 1]].reshape(1, -1).astype(f32)
    gain_one, shift_one, gain_two, shift_two, down_bias_full, up_bias_full = (
        part(i) for i in range(6)
    )
    table = part(6).reshape(NBUCKET, H)
    relative = table - table[NBUCKET - 1 :]
    reach = np.arange(256)
    bias = jnp.dot(
        relative.T, onehot_bucket(reach, reach < 129),
        precision=lax.Precision.HIGHEST, preferred_element_type=f32,
    ).reshape(8, 2, 256)

    scatter = lambda a: lax.psum_scatter(a, "fsdp", scatter_dimension=0, tiled=True)
    total = lambda a: lax.psum(a, "rep")

    if by_pieces:
        qkv_pieces = after_all(qkv_pieces, bias, gain_two)
        packed, normed, qkv_full = qkv_forward_pieces(me, tok, gain_one, shift_one, qkv_pieces)
    else:
        qkv_full = gather(w_qkv)
        packed, normed = qkv_forward(tok, gain_one, shift_one, qkv_full)

    def second(mine, other):
        a_send, a_keep, b_send, b_keep = core_sum(mine, other)
        return a_keep, swap(a_send, 2), b_keep, swap(b_send, 4)

    def third(parts):
        a_send, a_keep, b_send, b_keep = pair_sum(*parts)
        return a_keep, swap(a_send, 4), b_keep, swap(b_send, 2)

    place = lax.axis_index("rep").astype(jnp.int32).reshape(1)

    mixed, query_aug = attn_fwd(packed, bias, bound)
    down_full = gather(after(w_down, mixed, out_up))
    middle, normed_two = out_forward(mixed, out_up, tok, gain_two, shift_two)
    activ, slope = up_forward(normed_two, out_up, up_bias_full)
    grad_w_ffn = grad_down(activ, cot, ways)
    grad_pre, grad_up_bias = grad_pre_of(after(cot, grad_w_ffn), down_full, slope)
    grad_w_ffn = grad_up(normed_two, grad_pre, grad_w_ffn, ways)
    share_ffn = scatter(grad_w_ffn)
    grad_att, grad_mixed, grad_ffn_gain, grad_ffn_shift = grad_middle_of(
        after(grad_pre, grad_w_ffn), out_up, middle, cot, gain_two
    )
    low, reach_low = attn_bwd(packed, query_aug, mixed, grad_mixed, bias, bound, 0)
    if by_pieces:
        low_theirs, low_mine = grad_blocks(me, (normed, mixed), (low, grad_att))
        low_other = swap(low_theirs, 1)
        packed_next = after(packed, low_mine)
    else:
        packed_next = after(packed, low)
    high, reach_high = attn_bwd(packed_next, query_aug, mixed, grad_mixed, bias, bound, 1)
    grad_reach = jnp.concatenate([reach_low, reach_high], axis=0)
    near_hot = onehot_bucket(reach, reach < EDGES[-1])
    grad_near = jnp.dot(
        near_hot, grad_reach.reshape(H, 256).T,
        precision=lax.Precision.HIGHEST, preferred_element_type=f32,
    )
    far = (np.arange(NBUCKET) == NBUCKET - 1).astype(np.float32)[:, None]
    grad_rel_table = grad_near - far * jnp.sum(grad_near, axis=0, keepdims=True)
    if by_pieces:
        high_theirs, high_mine = grad_blocks(me, (normed,), (high,))
        high_other = swap(high_theirs, 1)
        high_next = after(high, high_mine)
    else:
        share_low = scatter(grad_columns(normed, low))
        share_high = scatter(grad_columns(normed, high))
        share_out = scatter(grad_columns(mixed, grad_att))
        high_next = high
    grad_tokens, grad_attn_gain, grad_attn_shift = grad_tokens_of(
        start, low, high_next, qkv_full, tok, grad_att, gain_one
    )
    sum_down, sum_up = widen(total(after(share_ffn, grad_tokens)))
    flat = lambda a: a.reshape(ways, -1)
    vectors = jnp.concatenate(
        [
            flat(grad_attn_gain), flat(grad_attn_shift), flat(grad_ffn_gain),
            flat(grad_ffn_shift), flat(grad_down_bias), flat(grad_up_bias), flat(grad_rel_table),
        ],
        axis=1,
    )
    activ_next = after(activ, grad_tokens)
    if by_pieces:
        for bit in (1, 2, 4):
            vectors = vectors + swap(vectors, bit)
        mine = lax.dynamic_slice_in_dim(vectors, lax.axis_index("fsdp"), 1, 0).reshape(-1)
        mine = jnp.concatenate([mine, jnp.zeros((128 * 128 - mine.size,), f32)])
        low_parts = second(after(low_mine, grad_tokens), low_other)
        high_parts = second(after(high_mine, low_parts[0]), high_other)
        low_parts = third(after_all(low_parts, high_parts[0]))
        high_parts = third(after_all(high_parts, low_parts[0]))
        send, keep = last_sum(
            place, mine.astype(bf16).reshape(128, 128), *low_parts, *high_parts
        )
        got = swap_rep(send, 1)
        activ_next = after(activ_next, keep)
    output = output_of(start, activ_next, down_full, middle, down_bias_full)
    if by_pieces:
        send, keep = half_sum(place, *after_all((keep, got), output))
        own = quarter_sum(after(keep, sum_up), swap_rep(send, 2))
        near = swap_rep(own, 2)
        far = jnp.concatenate([swap_rep(own, 1), swap_rep(own, 3)], axis=0)
        sum_qkv, sum_out, mine = spread(place, own, near, far)
        mine = mine.reshape(1, -1)
    else:
        mine = total(scatter(vectors))
        sum_out = total(share_out).astype(f32)
        sum_qkv = jnp.stack(
            [total(share_low).reshape(-1, 3, 512), total(share_high).reshape(-1, 3, 512)], axis=2
        ).reshape(-1, 3 * D).astype(f32)
    cut = lambda i: mine[0, cuts[i] : cuts[i + 1]].astype(f32)
    return (
        output, grad_tokens, cut(0), cut(1), sum_qkv, cut(6).reshape(-1, H),
        sum_out, cut(2), cut(3), sum_up, cut(5), sum_down, cut(4),
    )


def solution(mesh):
    rows, vec, mat = P(("rep", "fsdp"), None), P("fsdp"), P("fsdp", None)
    in_specs = (rows, rows, vec, vec, mat, mat, mat, vec, vec, mat, vec, mat, vec, rows)
    out_specs = (rows, rows, vec, vec, mat, mat, mat, vec, vec, mat, vec, mat, vec)
    return jax.shard_map(local, mesh=mesh, in_specs=in_specs, out_specs=out_specs, check_vma=False)
```
